128 devices in a mesh: row: 8 (over y, core), col: 16 (over x, z).
Axes of the slice: x: 4, y: 4, z: 4, core: 2. Of those that a mesh axis runs over, the one named last changes fastest.
Arguments:
- speech: bfloat16 [8192, 1024], P(('row', 'col')), may hold values from -16 to 16
- speech_mass: float32 [8192], P(('row', 'col')), may hold values from 0.2 to 15
- text: bfloat16 [16384, 1024], P('col', 'row'), may hold values from -16 to 16
- text_mass: float32 [16384], P('col'), may hold values from 0.2 to 15
Outputs:
- cross: float32 [1024, 1024], P(('row', 'col'))
- speech_potential: float32 [8192], P('row')
- text_potential: float32 [16384], P('col')
The draws below stay inside these ranges and needn't reach their ends.
All inputs are finite; a program needn't handle non-finite values.
Results may differ from the reference program's by a relative error of at most 0.015.
Values may be sent and summed in bfloat16 or wider, within the bound.
No kernel may reach another device: no remote copies, remote signals or barrier semaphores. Data moves between devices by JAX's collectives and lax.ppermute only.
A program may use at most 64 MiB of HBM per device.

```python
import jax
import jax.numpy as jnp
from jax import lax

D = 1024
S_DEV = 1024
ITERS = 3
NS = 8192
NT = 16384


def draw_speech(key, part):
    key = jax.random.fold_in(key, 1)
    first, second = jax.random.split(key)
    base = jnp.clip(jax.random.normal(first, (NS, D), jnp.float32), -6.0, 6.0)
    spread = jnp.exp(jax.random.uniform(second, (NS, 1), jnp.float32, -0.35, 0.35))
    result = base * spread
    return result.astype(jnp.bfloat16)


def draw_text(key, part):
    key = jax.random.fold_in(key, 2)
    first, second = jax.random.split(key)
    base = jnp.clip(jax.random.normal(first, (NT, D), jnp.float32), -6.0, 6.0)
    spread = jnp.exp(jax.random.uniform(second, (NT, 1), jnp.float32, -0.35, 0.35))
    result = base * spread
    return result.astype(jnp.bfloat16)


def draw_speech_mass(key, part):
    key = jax.random.fold_in(key, 3)
    trend = 1.0 + 2.0 * jnp.arange(NS, dtype=jnp.float32) / NS
    base = jnp.exp(jax.random.uniform(key, (NS,), jnp.float32, jnp.log(0.2), jnp.log(5.0)))
    return base * trend


def draw_text_mass(key, part):
    key = jax.random.fold_in(key, 4)
    trend = 1.0 + 2.0 * jnp.arange(NT, dtype=jnp.float32) / NT
    base = jnp.exp(jax.random.uniform(key, (NT,), jnp.float32, jnp.log(0.2), jnp.log(5.0)))
    return base * trend


def setup_inputs(seed: int = 0) -> dict:
    key_list = jax.random.split(jax.random.key(seed), 5)
    return {
        "speech": draw_speech(jax.random.fold_in(key_list[4], 71), 0),
        "speech_mass": draw_speech_mass(jax.random.fold_in(key_list[4], 71), 0),
        "text": draw_text(jax.random.fold_in(key_list[4], 71), 0),
        "text_mass": draw_text_mass(jax.random.fold_in(key_list[4], 71), 0),
    }


EPS = 0.5

def reference(speech, speech_mass, text, text_mass):
    width = speech.shape[1]
    scale = 1.0 / jnp.sqrt(jnp.float32(width))
    log_a = jnp.log(speech_mass) - jnp.log(jnp.sum(speech_mass))
    log_b = jnp.log(text_mass) - jnp.log(jnp.sum(text_mass))
    blocks = speech.reshape(-1, S_DEV, width)
    text_full = text.astype(jnp.float32)

    def cost_block(block):
        return -jnp.dot(block.astype(jnp.float32), text_full.T, precision=lax.Precision.HIGHEST) * scale
    cost = lax.map(cost_block, blocks)
    log_rows = log_a.reshape(-1, S_DEV)
    potential_s = jnp.zeros(log_rows.shape, jnp.float32)
    potential_t = jnp.zeros(log_b.shape, jnp.float32)
    for step in range(ITERS):
        scores = (potential_s[:, :, None] - cost) / EPS + log_rows[:, :, None]
        top = lax.optimization_barrier(jnp.max(scores, axis=(0, 1)))
        potential_t = -EPS * (top + jnp.log(lax.optimization_barrier(jnp.sum(jnp.exp(scores - top[None, None, :]), axis=(0, 1)))))
        scores = (potential_t[None, None, :] - cost) / EPS + log_b[None, None, :]
        top = lax.optimization_barrier(jnp.max(scores, axis=2))
        potential_s = -EPS * (top + jnp.log(lax.optimization_barrier(jnp.sum(jnp.exp(scores - top[:, :, None]), axis=2))))

    def carry_block(pieces):
        block_cost, block_pot, block_log = pieces
        plan = jnp.exp((block_pot[:, None] + potential_t[None, :] - block_cost) / EPS + block_log[:, None] + log_b[None, :])
        plan = plan.astype(jnp.bfloat16).astype(jnp.float32)
        return jnp.dot(plan, text_full, precision=lax.Precision.HIGHEST)
    carried = lax.map(carry_block, (cost, potential_s, log_rows)).reshape(-1, width)
    total_rows = speech.shape[0]
    cross = jnp.dot(speech.astype(jnp.float32).T, carried, precision=lax.Precision.HIGHEST)
    cross = cross * jnp.sqrt(jnp.float32(total_rows))
    return (cross, potential_s.reshape(-1), potential_t)
```

```python
import jax
import jax.numpy as jnp
from jax import lax
from jax.sharding import PartitionSpec as P

ITERS = 3
EPS = 0.5
LANES = 128


def three_terms(x):
    terms = []
    for _ in range(3):
        term = lax.reduce_precision(x, 8, 7)
        terms.append(term.astype(jnp.bfloat16))
        x = x - term
    return terms


def exchange(top, total, extra, axis):
    count = lax.axis_size(axis)
    rows = top.shape[0] // LANES
    piece = jnp.concatenate(
        [
            top.reshape(rows, LANES),
            total.reshape(rows, LANES),
            jnp.full((8, LANES), extra, jnp.float32),
        ],
        axis=0,
    )
    got = lax.all_to_all(jnp.broadcast_to(piece[None], (count,) + piece.shape), axis, 0, 0)
    tops, totals = got[:, :rows], got[:, rows : 2 * rows]
    best = jnp.max(tops, axis=0)
    mass = jnp.sum(totals * jnp.exp(tops - best[None]), axis=0)
    return best.reshape(-1), mass.reshape(-1), jnp.sum(got[:, 2 * rows, 0])


def body(speech, speech_mass, text, text_mass):
    rows, width = speech.shape
    columns = lax.axis_size("col")
    cores = 2
    block_text = lax.all_gather(text, "row", axis=1, tiled=True)
    tail = jnp.concatenate([t.reshape(1, rows) for t in three_terms(speech_mass)], axis=1)
    tail = jnp.pad(tail, ((0, 7), (0, width - tail.shape[1])))
    piece = jnp.concatenate([speech, tail], axis=0)
    got = lax.all_to_all(jnp.broadcast_to(piece[None], (columns,) + piece.shape), "col", 0, 0)
    block_speech = got[:, :rows].reshape(columns * rows, width)
    terms = got[:, rows].astype(jnp.float32)
    block_mass = (
        terms[:, :rows] + terms[:, rows : 2 * rows] + terms[:, 2 * rows : 3 * rows]
    ).reshape(-1)

    scale = 1.0 / (jnp.sqrt(jnp.float32(width)) * EPS)
    scores = scale * lax.dot_general(
        block_speech, block_text, (((1,), (1,)), ((), ())), preferred_element_type=jnp.float32
    )
    row_log, column_log = jnp.log(block_mass), jnp.log(text_mass)
    row_sum, column_sum = jnp.sum(block_mass), jnp.sum(text_mass)
    speech_dual = jnp.zeros_like(row_log)
    for step in range(ITERS):
        values = scores + (speech_dual + row_log)[:, None]
        top = jnp.max(values, axis=0)
        total = jnp.sum(jnp.exp(values - top[None, :]), axis=0)
        best, mass, speech_total = exchange(top, total, row_sum, "row")
        text_dual = jnp.log(speech_total) - (best + jnp.log(mass))
        values = scores + (text_dual + column_log)[None, :]
        top = jnp.max(values, axis=1)
        weights = jnp.exp(values - top[:, None])
        total = jnp.sum(weights, axis=1)
        best, mass, text_total = exchange(top, total, column_sum, "col")
        speech_dual = jnp.log(text_total) - (best + jnp.log(mass))
    carried = jnp.dot(weights.astype(jnp.bfloat16), block_text, preferred_element_type=jnp.float32)
    factor = (block_mass / speech_total) * jnp.exp(top - best) / mass
    carried = carried * factor[:, None]
    high = lax.reduce_precision(carried, 8, 7)
    low = (carried - high).astype(jnp.bfloat16)
    turn = (((0,), (0,)), ((), ()))
    cross = lax.dot_general(
        block_speech, high.astype(jnp.bfloat16), turn, preferred_element_type=jnp.float32
    ) + lax.dot_general(block_speech, low, turn, preferred_element_type=jnp.float32)

    row_count = lax.axis_size("row")
    here = lax.axis_index("row") % cores
    chips = row_count // cores
    out_rows = width // (row_count * columns)
    halves = cross.reshape(chips, cores, columns * out_rows, width)
    mine = lax.dynamic_index_in_dim(halves, here, 1, keepdims=False)
    other = lax.dynamic_index_in_dim(halves, 1 - here, 1, keepdims=False)
    other = lax.ppermute(
        other.astype(jnp.bfloat16), "row", [(i, i ^ 1) for i in range(row_count)]
    )
    pair = (mine + other.astype(jnp.float32)).astype(jnp.bfloat16)
    groups = [
        [r * columns + c for r in range(core, row_count, cores) for c in range(columns)]
        for core in range(cores)
    ]
    got = lax.all_to_all(
        pair.reshape(chips * columns, out_rows, width),
        ("row", "col"),
        0,
        0,
        axis_index_groups=groups,
    )
    cross = jnp.sum(got.astype(jnp.float32), axis=0)
    cross = cross * jnp.sqrt(jnp.float32(block_speech.shape[0] * row_count))
    return (cross, EPS * speech_dual, EPS * text_dual)


def solution(mesh):
    return jax.shard_map(
        body,
        mesh=mesh,
        in_specs=(P(("row", "col"), None), P(("row", "col")), P("col", "row"), P("col")),
        out_specs=(P(("row", "col"), None), P("row"), P("col")),
        check_vma=False,
    )
```

```python
import math

import jax
import jax.numpy as jnp
from jax import lax
from jax.experimental import pallas as pl
from jax.experimental.pallas import tpu as pltpu
from jax.sharding import PartitionSpec as P

ITERS = 3
EPS = 0.5
LANES = 128
SUB = 8
LOG2E = math.log2(math.e)
LIMIT = 36 * 1024 * 1024


def call(kernel, outs, scratch=(), flops=0, reads=0, scalars=0, args=0):
    vmem = pl.BlockSpec(memory_space=pltpu.VMEM)
    smem = pl.BlockSpec(memory_space=pltpu.SMEM)
    return pl.pallas_call(
        kernel,
        out_shape=outs,
        in_specs=[smem] * scalars + [vmem] * args,
        out_specs=[vmem] * len(outs),
        scratch_shapes=list(scratch),
        compiler_params=pltpu.CompilerParams(vmem_limit_bytes=LIMIT),
        cost_estimate=pl.CostEstimate(flops=flops, bytes_accessed=reads, transcendentals=0),
    )


def f32(*shape):
    return jax.ShapeDtypeStruct(shape, jnp.float32)


def bf16(*shape):
    return jax.ShapeDtypeStruct(shape, jnp.bfloat16)


def total_of(x):
    return jnp.sum(jnp.sum(x, axis=1, keepdims=True), axis=0, keepdims=True)


def combine(got_ref):
    tops = got_ref[:, 0:SUB, :]
    best = jnp.max(tops, axis=0)
    mass = jnp.sum(got_ref[:, SUB : 2 * SUB, :] * jnp.exp2(tops - best[None]), axis=0)
    whole = jnp.sum(got_ref[:, 2 * SUB : 3 * SUB, :], axis=0)
    return best, mass, whole


def send(out_ref, top, mass, whole):
    whole = jnp.broadcast_to(whole, (SUB, LANES))
    for peer in range(out_ref.shape[0]):
        out_ref[peer, 0:SUB, :] = top
        out_ref[peer, SUB : 2 * SUB, :] = mass
        out_ref[peer, 2 * SUB : 3 * SUB, :] = whole


def spread(v, out_ref):
    turned = jnp.concatenate([v, jnp.zeros((LANES - SUB, LANES), jnp.float32)], axis=0).T
    for b in range(SUB):
        out_ref[b * LANES : (b + 1) * LANES, :] = jnp.broadcast_to(
            turned[:, b : b + 1], (LANES, LANES)
        )


def column_stats(scores_ref, rows_ref, top_ref, mass_ref):
    for b in range(SUB):
        values = scores_ref[:, b * LANES : (b + 1) * LANES] + rows_ref[...]
        top = jnp.max(values, axis=0, keepdims=True)
        mass = jnp.sum(jnp.exp2(values - top), axis=0, keepdims=True)
        top_ref[b : b + 1, :] = top
        mass_ref[b : b + 1, :] = mass


def row_stats(scores_ref, v, weights_ref=None):
    lane = lax.broadcasted_iota(jnp.int32, (LANES, LANES), 1)
    shift = jnp.concatenate([v[b : b + 1, :] for b in range(SUB)], axis=1)
    both = jnp.zeros((LANES, LANES), jnp.float32)
    for b in range(SUB):
        values = scores_ref[b * LANES : (b + 1) * LANES, :] + shift
        top = jnp.max(values, axis=1, keepdims=True)
        weights = jnp.exp2(values - top)
        mass = jnp.sum(weights, axis=1, keepdims=True)
        if weights_ref is not None:
            weights_ref[b * LANES : (b + 1) * LANES, :] = weights.astype(jnp.bfloat16)
        both = jnp.where(lane == b, top, both)
        both = jnp.where(lane == SUB + b, mass, both)
    turned = both.T
    return turned[0:SUB, :], turned[SUB : 2 * SUB, :]


def gram_kernel(scale, rows, x_ref, t_ref, scores_ref, s_ref, mass_ref, out_ref, rows_ref, a_ref, b_ref):
    blocks, _, _ = t_ref.shape
    peers = x_ref.shape[0]
    for c in range(peers):
        for lt in range(blocks):
            s_ref[lt, c * rows : (c + 1) * rows, :] = x_ref[c, lt * rows : (lt + 1) * rows, :]
    lane = lax.broadcasted_iota(jnp.int32, (1, LANES), 1)
    base = blocks * rows
    for b in range(SUB):
        pair = []
        for c in (2 * b, 2 * b + 1):
            terms = x_ref[c, base : base + 16, :].astype(jnp.float32)
            pair.append(terms[0:1, :] + terms[1:2, :] + terms[2:3, :])
        mass_ref[b : b + 1, :] = jnp.where(lane < rows, pair[0], pair[1])
    mass = mass_ref[...]
    spread(jnp.log2(mass), rows_ref)
    whole = jnp.concatenate([s_ref[lt] for lt in range(blocks)], axis=1)
    for n in range(4):
        text = jnp.concatenate([t_ref[lt, n * 256 : (n + 1) * 256, :] for lt in range(blocks)], axis=1)
        product = lax.dot_general(
            whole, text, (((1,), (1,)), ((), ())), preferred_element_type=jnp.float32
        )
        scores_ref[:, n * 256 : (n + 1) * 256] = product * scale
    column_stats(scores_ref, rows_ref, a_ref, b_ref)
    send(out_ref, a_ref[...], b_ref[...], total_of(mass))


def row_kernel(got_ref, scores_ref, mass_ref, out_ref):
    best, mass, whole = combine(got_ref)
    dual = jnp.log2(whole) - (best + jnp.log2(mass))
    top, mass = row_stats(scores_ref, dual + jnp.log2(mass_ref[...]))
    send(out_ref, top, mass, total_of(mass_ref[...]))


def last_row_kernel(got_ref, scores_ref, mass_ref, out_ref, weights_ref, dual_ref):
    best, mass, whole = combine(got_ref)
    dual = jnp.log2(whole) - (best + jnp.log2(mass))
    dual_ref[...] = dual * (EPS / LOG2E)
    top, mass = row_stats(scores_ref, dual + jnp.log2(mass_ref[...]), weights_ref)
    send(out_ref, top, mass, total_of(mass_ref[...]))


def column_kernel(got_ref, scores_ref, mass_ref, out_ref, rows_ref, a_ref, b_ref):
    best, mass, whole = combine(got_ref)
    dual = jnp.log2(whole) - (best + jnp.log2(mass))
    spread(dual + jnp.log2(mass_ref[...]), rows_ref)
    column_stats(scores_ref, rows_ref, a_ref, b_ref)
    send(out_ref, a_ref[...], b_ref[...], total_of(mass_ref[...]))


def carry_kernel(weights_ref, t_ref, out_ref):
    for n in range(4):
        text = jnp.concatenate([t_ref[2 * n], t_ref[2 * n + 1]], axis=1)
        out_ref[:, n * 256 : (n + 1) * 256] = jnp.dot(
            weights_ref[...], text, preferred_element_type=jnp.float32
        )


def half_cross(s_ref, part, carried_ref, p):
    left = jnp.concatenate([s_ref[4 * p + part], s_ref[4 * p + 2 + part]], axis=1)
    return lax.dot_general(
        left, carried_ref[...], (((0,), (0,)), ((), ())), preferred_element_type=jnp.float32
    )


def first_cross_kernel(
    here_ref, got_ref, sent_ref, row_got_ref, mass_ref, raw_ref, s_ref,
    carried_ref, other_ref, dual_ref, rows_ref,
):
    best, mass, whole = combine(got_ref)
    dual_ref[...] = (jnp.log2(whole) - (best + jnp.log2(mass))) * (EPS / LOG2E)
    speech_total = jnp.sum(row_got_ref[:, 2 * SUB : 3 * SUB, :], axis=0)
    factor = (mass_ref[...] / speech_total) * jnp.exp2(sent_ref[0, 0:SUB, :] - best) / mass
    spread(factor, rows_ref)
    for b in range(SUB):
        carried_ref[:, b * LANES : (b + 1) * LANES] = (
            raw_ref[:, b * LANES : (b + 1) * LANES] * rows_ref[...]
        ).astype(jnp.bfloat16)
    part = 1 - here_ref[0]
    for p in range(2):
        other_ref[p * 256 : (p + 1) * 256, :] = half_cross(s_ref, part, carried_ref, p).astype(
            jnp.bfloat16
        )


def second_cross_kernel(here_ref, carried_ref, s_ref, other_ref, out_ref):
    part = here_ref[0]
    for p in range(2):
        rows = slice(p * 256, (p + 1) * 256)
        out_ref[rows, :] = (
            half_cross(s_ref, part, carried_ref, p) + other_ref[rows, :].astype(jnp.float32)
        ).astype(jnp.bfloat16)


def three_terms(x):
    terms = []
    for _ in range(3):
        term = lax.reduce_precision(x, 8, 7)
        terms.append(term.astype(jnp.bfloat16))
        x = x - term
    return terms


def to_all(piece, axis):
    count = lax.axis_size(axis)
    return lax.all_to_all(jnp.broadcast_to(piece[None], (count,) + piece.shape), axis, 0, 0)


def body(speech, speech_mass, text, text_mass):
    rows, width = speech.shape
    columns, row_count = lax.axis_size("col"), lax.axis_size("row")
    cores = 2
    blocks = width // LANES
    big = columns * rows
    flops = 2 * big * big * width

    t = to_all(text, "row")
    terms = jnp.stack(three_terms(speech_mass))
    tail = jnp.pad(jnp.concatenate([terms, terms], axis=1), ((0, 13), (0, 0)))
    lanes_first = speech.reshape(rows, blocks, LANES).transpose(1, 0, 2).reshape(-1, LANES)
    x = to_all(jnp.concatenate([lanes_first, tail], axis=0), "col")
    column_mass = text_mass.reshape(SUB, LANES)

    scale = LOG2E / (math.sqrt(width) * EPS)
    vector = pltpu.VMEM((SUB, LANES), jnp.float32)
    column = pltpu.VMEM((big, LANES), jnp.float32)
    scores, s, row_mass, piece = call(
        lambda *refs: gram_kernel(scale, rows, *refs),
        [f32(big, big), bf16(blocks, big, LANES), f32(SUB, LANES), f32(row_count, 24, LANES)],
        [column, vector, vector],
        flops=flops,
        args=2,
    )(x, t)
    row_swap = lambda v: lax.all_to_all(v, "row", 0, 0)
    column_swap = lambda v: lax.all_to_all(v, "col", 0, 0)
    for step in range(ITERS):
        got_row = row_swap(piece)
        if step < ITERS - 1:
            (piece,) = call(row_kernel, [f32(columns, 24, LANES)], args=3)(
                got_row, scores, column_mass
            )
            got = column_swap(piece)
            (piece,) = call(
                column_kernel, [f32(row_count, 24, LANES)], [column, vector, vector], args=3
            )(got, scores, row_mass)
    sent, weights, text_dual = call(
        last_row_kernel,
        [f32(columns, 24, LANES), bf16(big, big), f32(SUB, LANES)],
        args=3,
    )(got_row, scores, column_mass)
    got = column_swap(sent)
    (raw,) = call(carry_kernel, [f32(big, width)], flops=flops, args=2)(weights, t)
    here = (lax.axis_index("row") % cores).astype(jnp.int32).reshape(1)
    carried, other, speech_dual = call(
        first_cross_kernel,
        [bf16(big, width), bf16(width // 2, width), f32(SUB, LANES)],
        [column],
        flops=flops // 2,
        scalars=1,
        args=6,
    )(here, got, sent, got_row, row_mass, raw, s)
    other = lax.ppermute(other, "row", [(i, i ^ 1) for i in range(row_count)])
    (pair,) = call(
        second_cross_kernel, [bf16(width // 2, width)], flops=flops // 2, scalars=1, args=3
    )(here, carried, s, other)
    groups = [
        [r * columns + c for r in range(core, row_count, cores) for c in range(columns)]
        for core in range(cores)
    ]
    count = len(groups[0])
    parts = lax.all_to_all(
        pair.reshape(count, width // 2 // count, width),
        ("row", "col"),
        0,
        0,
        axis_index_groups=groups,
    )
    cross = jnp.sum(parts.astype(jnp.float32), axis=0) * math.sqrt(big * row_count)
    return (cross, speech_dual.reshape(-1), text_dual.reshape(-1))


def solution(mesh):
    return jax.shard_map(
        body,
        mesh=mesh,
        in_specs=(P(("row", "col"), None), P(("row", "col")), P("col", "row"), P("col")),
        out_specs=(P(("row", "col"), None), P("row"), P("col")),
        check_vma=False,
    )
```

```python
import math

import jax
import jax.numpy as jnp
from jax import lax
from jax.experimental import pallas as pl
from jax.experimental.pallas import tpu as pltpu
from jax.sharding import PartitionSpec as P

ITERS = 3
EPS = 0.5
LANES = 128
SUB = 8
LOG2E = math.log2(math.e)
LIMIT = 24 * 1024 * 1024


def call(kernel, outs, scratch=(), flops=0, reads=0, args=0):
    vmem = pl.BlockSpec(memory_space=pltpu.VMEM)
    return pl.pallas_call(
        kernel,
        out_shape=outs,
        in_specs=[vmem] * args,
        out_specs=[vmem] * len(outs),
        scratch_shapes=list(scratch),
        compiler_params=pltpu.CompilerParams(vmem_limit_bytes=LIMIT),
        cost_estimate=pl.CostEstimate(flops=flops, bytes_accessed=reads, transcendentals=0),
    )


def f32(*shape):
    return jax.ShapeDtypeStruct(shape, jnp.float32)


def bf16(*shape):
    return jax.ShapeDtypeStruct(shape, jnp.bfloat16)


def total_of(x):
    return jnp.sum(jnp.sum(x, axis=1, keepdims=True), axis=0, keepdims=True)


def combine(got_ref):
    tops = got_ref[:, 0:SUB, :]
    best = jnp.max(tops, axis=0)
    mass = jnp.sum(got_ref[:, SUB : 2 * SUB, :] * jnp.exp2(tops - best[None]), axis=0)
    whole = jnp.sum(got_ref[:, 2 * SUB : 3 * SUB, :], axis=0)
    return best, mass, whole


def send(out_ref, top, mass, whole):
    whole = jnp.broadcast_to(whole, (SUB, LANES))
    for peer in range(out_ref.shape[0]):
        out_ref[peer, 0:SUB, :] = top
        out_ref[peer, SUB : 2 * SUB, :] = mass
        out_ref[peer, 2 * SUB : 3 * SUB, :] = whole


def spread(v, out_ref):
    turned = jnp.concatenate([v, jnp.zeros((LANES - SUB, LANES), jnp.float32)], axis=0).T
    for b in range(SUB):
        out_ref[b * LANES : (b + 1) * LANES, :] = jnp.broadcast_to(
            turned[:, b : b + 1], (LANES, LANES)
        )


def column_stats(scores_ref, rows_ref, top_ref, mass_ref):
    for b in range(SUB):
        values = scores_ref[:, b * LANES : (b + 1) * LANES] + rows_ref[...]
        top = jnp.max(values, axis=0, keepdims=True)
        mass = jnp.sum(jnp.exp2(values - top), axis=0, keepdims=True)
        top_ref[b : b + 1, :] = top
        mass_ref[b : b + 1, :] = mass


def row_stats(scores_ref, v, weights_ref=None):
    lane = lax.broadcasted_iota(jnp.int32, (LANES, LANES), 1)
    shift = jnp.concatenate([v[b : b + 1, :] for b in range(SUB)], axis=1)
    both = jnp.zeros((LANES, LANES), jnp.float32)
    for b in range(SUB):
        values = scores_ref[b * LANES : (b + 1) * LANES, :] + shift
        top = jnp.max(values, axis=1, keepdims=True)
        weights = jnp.exp2(values - top)
        mass = jnp.sum(weights, axis=1, keepdims=True)
        if weights_ref is not None:
            weights_ref[b * LANES : (b + 1) * LANES, :] = weights.astype(jnp.bfloat16)
        both = jnp.where(lane == b, top, both)
        both = jnp.where(lane == SUB + b, mass, both)
    turned = both.T
    return turned[0:SUB, :], turned[SUB : 2 * SUB, :]


def pack_kernel(speech_ref, mass_ref, out_ref):
    peers = out_ref.shape[0]
    rows, width = speech_ref.shape
    blocks = width // LANES
    rest = jnp.concatenate([mass_ref[...], mass_ref[...]], axis=1)
    line = lax.broadcasted_iota(jnp.int32, (16, LANES), 0)
    tail = jnp.zeros((16, LANES), jnp.float32)
    for k in range(3):
        term = rest.astype(jnp.bfloat16).astype(jnp.float32)
        tail = jnp.where(line == k, term, tail)
        rest = rest - term
    tail = tail.astype(jnp.bfloat16)
    for c in range(peers):
        for lt in range(blocks):
            out_ref[c, lt * rows : (lt + 1) * rows, :] = speech_ref[:, lt * LANES : (lt + 1) * LANES]
        out_ref[c, blocks * rows :, :] = tail


def gram_kernel(
    scale, rows, x_ref, own_ref, *refs
):
    other_refs = refs[:7]
    scores_ref, s_ref, t_ref, mass_ref, out_ref, rows_ref, a_ref, b_ref = refs[7:]
    blocks = t_ref.shape[0]
    peers = x_ref.shape[0]
    here = lax.axis_index("row")
    t_ref[here] = own_ref[...]
    for k in range(1, blocks):
        t_ref[lax.rem(here // 2 + blocks // 2 - k // 2, blocks // 2) * 2 + lax.rem(here + k, 2)] = (
            other_refs[k - 1][...]
        )
    for c in range(peers):
        for lt in range(blocks):
            s_ref[lt, c * rows : (c + 1) * rows, :] = x_ref[c, lt * rows : (lt + 1) * rows, :]
    lane = lax.broadcasted_iota(jnp.int32, (1, LANES), 1)
    base = blocks * rows
    for b in range(SUB):
        pair = []
        for c in (2 * b, 2 * b + 1):
            terms = x_ref[c, base : base + 16, :].astype(jnp.float32)
            pair.append(terms[0:1, :] + terms[1:2, :] + terms[2:3, :])
        mass_ref[b : b + 1, :] = jnp.where(lane < rows, pair[0], pair[1])
    mass = mass_ref[...]
    spread(jnp.log2(mass), rows_ref)
    whole = jnp.concatenate([s_ref[lt] for lt in range(blocks)], axis=1)
    for n in range(4):
        text = jnp.concatenate([t_ref[lt, n * 256 : (n + 1) * 256, :] for lt in range(blocks)], axis=1)
        product = lax.dot_general(
            whole, text, (((1,), (1,)), ((), ())), preferred_element_type=jnp.float32
        )
        scores_ref[:, n * 256 : (n + 1) * 256] = product * scale
    column_stats(scores_ref, rows_ref, a_ref, b_ref)
    send(out_ref, a_ref[...], b_ref[...], total_of(mass))


def row_kernel(got_ref, scores_ref, mass_ref, out_ref):
    best, mass, whole = combine(got_ref)
    dual = jnp.log2(whole) - (best + jnp.log2(mass))
    top, mass = row_stats(scores_ref, dual + jnp.log2(mass_ref[...]))
    send(out_ref, top, mass, total_of(mass_ref[...]))


def last_row_kernel(
    got_ref, scores_ref, mass_ref, t_ref, out_ref, raw_ref, dual_ref, weights_ref
):
    best, mass, whole = combine(got_ref)
    dual = jnp.log2(whole) - (best + jnp.log2(mass))
    dual_ref[...] = dual * (EPS / LOG2E)
    top, mass = row_stats(scores_ref, dual + jnp.log2(mass_ref[...]), weights_ref)
    send(out_ref, top, mass, total_of(mass_ref[...]))
    for n in range(4):
        text = jnp.concatenate([t_ref[2 * n], t_ref[2 * n + 1]], axis=1)
        raw_ref[:, n * 256 : (n + 1) * 256] = jnp.dot(
            weights_ref[...], text, preferred_element_type=jnp.float32
        )


def column_kernel(got_ref, scores_ref, mass_ref, out_ref, rows_ref, a_ref, b_ref):
    best, mass, whole = combine(got_ref)
    dual = jnp.log2(whole) - (best + jnp.log2(mass))
    spread(dual + jnp.log2(mass_ref[...]), rows_ref)
    column_stats(scores_ref, rows_ref, a_ref, b_ref)
    send(out_ref, a_ref[...], b_ref[...], total_of(mass_ref[...]))


def half_cross(s_ref, part, carried_ref, p):
    left = jnp.concatenate([s_ref[4 * p + part], s_ref[4 * p + 2 + part]], axis=1)
    return lax.dot_general(
        left, carried_ref[...], (((0,), (0,)), ((), ())), preferred_element_type=jnp.float32
    )


def first_cross_kernel(
    got_ref, sent_ref, row_got_ref, mass_ref, raw_ref, s_ref,
    carried_ref, other_ref, dual_ref, rows_ref,
):
    best, mass, whole = combine(got_ref)
    dual_ref[...] = (jnp.log2(whole) - (best + jnp.log2(mass))) * (EPS / LOG2E)
    speech_total = jnp.sum(row_got_ref[:, 2 * SUB : 3 * SUB, :], axis=0)
    factor = (mass_ref[...] / speech_total) * jnp.exp2(sent_ref[0, 0:SUB, :] - best) / mass
    spread(factor, rows_ref)
    for b in range(SUB):
        carried_ref[:, b * LANES : (b + 1) * LANES] = (
            raw_ref[:, b * LANES : (b + 1) * LANES] * rows_ref[...]
        ).astype(jnp.bfloat16)
    part = 1 - lax.rem(lax.axis_index("row"), 2)
    for p in range(2):
        other_ref[p * 256 : (p + 1) * 256, :] = half_cross(s_ref, part, carried_ref, p).astype(
            jnp.bfloat16
        )


def second_cross_kernel(carried_ref, s_ref, other_ref, out_ref):
    part = lax.rem(lax.axis_index("row"), 2)
    for p in range(2):
        rows = slice(p * 256, (p + 1) * 256)
        out_ref[rows, :] = (
            half_cross(s_ref, part, carried_ref, p) + other_ref[rows, :].astype(jnp.float32)
        ).astype(jnp.bfloat16)


def body(speech, speech_mass, text, text_mass):
    rows, width = speech.shape
    columns, row_count = lax.axis_size("col"), lax.axis_size("row")
    cores = 2
    blocks = width // LANES
    big = columns * rows
    flops = 2 * big * big * width

    slices = [text] + [
        lax.ppermute(text, "row", [(i, (i + cores * k) % row_count) for i in range(row_count)])
        for k in range(1, row_count // cores)
    ]
    swap = [(i, i ^ 1) for i in range(row_count)]
    slices = [v for piece in slices for v in (piece, lax.ppermute(piece, "row", swap))]
    (x,) = call(pack_kernel, [bf16(columns, blocks * rows + 16, LANES)], args=2)(
        speech, speech_mass.reshape(1, rows)
    )
    x = lax.all_to_all(x, "col", 0, 0)
    column_mass = text_mass.reshape(SUB, LANES)

    scale = LOG2E / (math.sqrt(width) * EPS)
    vector = pltpu.VMEM((SUB, LANES), jnp.float32)
    column = pltpu.VMEM((big, LANES), jnp.float32)
    scores, s, t, row_mass, piece = call(
        lambda *refs: gram_kernel(scale, rows, *refs),
        [
            f32(big, big),
            bf16(blocks, big, LANES),
            bf16(blocks, big, LANES),
            f32(SUB, LANES),
            f32(row_count, 24, LANES),
        ],
        [column, vector, vector],
        flops=flops,
        args=1 + row_count,
    )(x, *slices)
    row_swap = lambda v: lax.all_to_all(v, "row", 0, 0)
    column_swap = lambda v: lax.all_to_all(v, "col", 0, 0)
    for step in range(ITERS):
        got_row = row_swap(piece)
        if step < ITERS - 1:
            (piece,) = call(row_kernel, [f32(columns, 24, LANES)], args=3)(
                got_row, scores, column_mass
            )
            got = column_swap(piece)
            (piece,) = call(
                column_kernel, [f32(row_count, 24, LANES)], [column, vector, vector], args=3
            )(got, scores, row_mass)
    sent, raw, text_dual = call(
        last_row_kernel,
        [f32(columns, 24, LANES), f32(big, width), f32(SUB, LANES)],
        [pltpu.VMEM((big, big), jnp.bfloat16)],
        flops=flops,
        args=4,
    )(got_row, scores, column_mass, t)
    got = column_swap(sent)
    carried, other, speech_dual = call(
        first_cross_kernel,
        [bf16(big, width), bf16(width // 2, width), f32(SUB, LANES)],
        [column],
        flops=flops // 2,
        args=6,
    )(got, sent, got_row, row_mass, raw, s)
    other = lax.ppermute(other, "row", swap)
    (pair,) = call(
        second_cross_kernel, [bf16(width // 2, width)], flops=flops // 2, args=3
    )(carried, s, other)
    groups = [
        [r * columns + c for r in range(core, row_count, cores) for c in range(columns)]
        for core in range(cores)
    ]
    count = len(groups[0])
    parts = lax.all_to_all(
        pair.reshape(count, width // 2 // count, width),
        ("row", "col"),
        0,
        0,
        axis_index_groups=groups,
    )
    cross = jnp.sum(parts.astype(jnp.float32), axis=0) * math.sqrt(big * row_count)
    return (cross, speech_dual.reshape(-1), text_dual.reshape(-1))


def solution(mesh):
    return jax.shard_map(
        body,
        mesh=mesh,
        in_specs=(P(("row", "col"), None), P(("row", "col")), P("col", "row"), P("col")),
        out_specs=(P(("row", "col"), None), P("row"), P("col")),
        check_vma=False,
    )
```

```python
import math

import jax
import jax.numpy as jnp
from jax import lax
from jax.experimental import pallas as pl
from jax.experimental.pallas import tpu as pltpu
from jax.sharding import PartitionSpec as P

ITERS = 3
EPS = 0.5
LANES = 128
SUB = 8
LOG2E = math.log2(math.e)
LIMIT = 24 * 1024 * 1024


def call(kernel, outs, scratch=(), flops=0, reads=0, args=0, far_args=0, far_out=False):
    vmem = pl.BlockSpec(memory_space=pltpu.VMEM)
    far = pl.BlockSpec(memory_space=pl.ANY)
    return pl.pallas_call(
        kernel,
        out_shape=outs,
        in_specs=[vmem] * args + [far] * far_args,
        out_specs=[far if far_out else vmem] * len(outs),
        scratch_shapes=list(scratch),
        compiler_params=pltpu.CompilerParams(vmem_limit_bytes=LIMIT),
        cost_estimate=pl.CostEstimate(flops=flops, bytes_accessed=reads, transcendentals=0),
    )


def f32(*shape):
    return jax.ShapeDtypeStruct(shape, jnp.float32)


def bf16(*shape):
    return jax.ShapeDtypeStruct(shape, jnp.bfloat16)


def total_of(x):
    return jnp.sum(jnp.sum(x, axis=1, keepdims=True), axis=0, keepdims=True)


def combine(got_ref):
    tops = got_ref[:, 0:SUB, :]
    best = jnp.max(tops, axis=0)
    mass = jnp.sum(got_ref[:, SUB : 2 * SUB, :] * jnp.exp2(tops - best[None]), axis=0)
    whole = jnp.sum(got_ref[:, 2 * SUB : 3 * SUB, :], axis=0)
    return best, mass, whole


def send(out_ref, top, mass, whole):
    whole = jnp.broadcast_to(whole, (SUB, LANES))
    for peer in range(out_ref.shape[0]):
        out_ref[peer, 0:SUB, :] = top
        out_ref[peer, SUB : 2 * SUB, :] = mass
        out_ref[peer, 2 * SUB : 3 * SUB, :] = whole


def spread(v, out_ref):
    turned = jnp.concatenate([v, jnp.zeros((LANES - SUB, LANES), jnp.float32)], axis=0).T
    for b in range(SUB):
        out_ref[b * LANES : (b + 1) * LANES, :] = jnp.broadcast_to(
            turned[:, b : b + 1], (LANES, LANES)
        )


def column_stats(scores_ref, rows_ref, top_ref, mass_ref, blocks=range(SUB)):
    for b in blocks:
        values = scores_ref[:, b * LANES : (b + 1) * LANES] + rows_ref[...]
        top = jnp.max(values, axis=0, keepdims=True)
        mass = jnp.sum(jnp.exp2(values - top), axis=0, keepdims=True)
        top_ref[b : b + 1, :] = top
        mass_ref[b : b + 1, :] = mass


def row_stats(scores_ref, v, use=None):
    lane = lax.broadcasted_iota(jnp.int32, (LANES, LANES), 1)
    shift = jnp.concatenate([v[b : b + 1, :] for b in range(SUB)], axis=1)
    both = jnp.zeros((LANES, LANES), jnp.float32)
    for b in range(SUB):
        values = scores_ref[b * LANES : (b + 1) * LANES, :] + shift
        top = jnp.max(values, axis=1, keepdims=True)
        weights = jnp.exp2(values - top)
        mass = jnp.sum(weights, axis=1, keepdims=True)
        if use is not None:
            use(b, weights)
        both = jnp.where(lane == b, top, both)
        both = jnp.where(lane == SUB + b, mass, both)
    turned = both.T
    return turned[0:SUB, :], turned[SUB : 2 * SUB, :]


def pack_kernel(speech_ref, mass_ref, out_ref, held_ref, mass_held_ref, piece_ref, in_sems, sems):
    peers = out_ref.shape[0]
    rows, width = speech_ref.shape
    blocks = width // LANES
    loads = [
        pltpu.make_async_copy(speech_ref, held_ref, in_sems.at[0]),
        pltpu.make_async_copy(mass_ref, mass_held_ref, in_sems.at[1]),
    ]
    for load in loads:
        load.start()
    for load in loads:
        load.wait()
    rest = jnp.concatenate([mass_held_ref[...], mass_held_ref[...]], axis=1)
    line = lax.broadcasted_iota(jnp.int32, (16, LANES), 0)
    tail = jnp.zeros((16, LANES), jnp.float32)
    for k in range(3):
        term = rest.astype(jnp.bfloat16).astype(jnp.float32)
        tail = jnp.where(line == k, term, tail)
        rest = rest - term
    for lt in range(blocks):
        piece_ref[lt * rows : (lt + 1) * rows, :] = held_ref[:, lt * LANES : (lt + 1) * LANES]
    piece_ref[blocks * rows :, :] = tail.astype(jnp.bfloat16)
    stores = [pltpu.make_async_copy(piece_ref, out_ref.at[c], sems.at[c]) for c in range(peers)]
    for store in stores:
        store.start()
    for store in stores:
        store.wait()


def gram_kernel(scale, rows, x_ref, *refs):
    slice_refs = refs[:8]
    scores_ref, s_ref, t_ref, mass_ref, out_ref, rows_ref, a_ref, b_ref, sems = refs[8:]
    blocks = t_ref.shape[0]
    peers = x_ref.shape[0]
    here = lax.axis_index("row")
    chips = blocks // 2
    loads = []
    for k in range(blocks):
        block = lax.rem(here // 2 + chips - k // 2, chips) * 2 + lax.rem(here + k, 2)
        loads.append(pltpu.make_async_copy(slice_refs[k], t_ref.at[block], sems.at[k]))
        loads[-1].start()
    for c in range(peers):
        for lt in range(blocks):
            s_ref[lt, c * rows : (c + 1) * rows, :] = x_ref[c, lt * rows : (lt + 1) * rows, :]
    lane = lax.broadcasted_iota(jnp.int32, (1, LANES), 1)
    base = blocks * rows
    for b in range(SUB):
        pair = []
        for c in (2 * b, 2 * b + 1):
            terms = x_ref[c, base : base + 16, :].astype(jnp.float32)
            pair.append(terms[0:1, :] + terms[1:2, :] + terms[2:3, :])
        mass_ref[b : b + 1, :] = jnp.where(lane < rows, pair[0], pair[1])
    mass = mass_ref[...]
    spread(jnp.log2(mass), rows_ref)
    whole = jnp.concatenate([s_ref[lt] for lt in range(blocks)], axis=1)
    for load in loads:
        load.wait()
    for n in range(4):
        text = jnp.concatenate([t_ref[lt, n * 256 : (n + 1) * 256, :] for lt in range(blocks)], axis=1)
        product = lax.dot_general(
            whole, text, (((1,), (1,)), ((), ())), preferred_element_type=jnp.float32
        )
        scores_ref[:, n * 256 : (n + 1) * 256] = product * scale
        column_stats(scores_ref, rows_ref, a_ref, b_ref, (2 * n, 2 * n + 1))
    send(out_ref, a_ref[...], b_ref[...], total_of(mass))


def row_kernel(got_ref, scores_ref, mass_ref, out_ref):
    best, mass, whole = combine(got_ref)
    dual = jnp.log2(whole) - (best + jnp.log2(mass))
    top, mass = row_stats(scores_ref, dual + jnp.log2(mass_ref[...]))
    send(out_ref, top, mass, total_of(mass_ref[...]))


def last_row_kernel(
    got_ref, scores_ref, mass_ref, t_ref, out_ref, raw_ref, dual_ref, weights_ref
):
    best, mass, whole = combine(got_ref)
    dual = jnp.log2(whole) - (best + jnp.log2(mass))
    dual_ref[...] = dual * (EPS / LOG2E)

    def use(b, weights):
        rows = slice(b * LANES, (b + 1) * LANES)
        weights_ref[rows, :] = weights.astype(jnp.bfloat16)
        if b % 2 == 0:
            return
        rows = slice((b - 1) * LANES, (b + 1) * LANES)
        text = jnp.concatenate([t_ref[lt] for lt in range(t_ref.shape[0])], axis=1)
        raw_ref[rows, :] = jnp.dot(weights_ref[rows, :], text, preferred_element_type=jnp.float32)

    top, mass = row_stats(scores_ref, dual + jnp.log2(mass_ref[...]), use)
    send(out_ref, top, mass, total_of(mass_ref[...]))


def column_kernel(got_ref, scores_ref, mass_ref, out_ref, rows_ref, a_ref, b_ref):
    best, mass, whole = combine(got_ref)
    dual = jnp.log2(whole) - (best + jnp.log2(mass))
    spread(dual + jnp.log2(mass_ref[...]), rows_ref)
    column_stats(scores_ref, rows_ref, a_ref, b_ref)
    send(out_ref, a_ref[...], b_ref[...], total_of(mass_ref[...]))


def half_cross(s_ref, part, carried_ref, p):
    left = jnp.concatenate([s_ref[4 * p + part], s_ref[4 * p + 2 + part]], axis=1)
    return lax.dot_general(
        left, carried_ref[...], (((0,), (0,)), ((), ())), preferred_element_type=jnp.float32
    )


def first_cross_kernel(
    got_ref, sent_ref, row_got_ref, mass_ref, raw_ref, s_ref,
    carried_ref, other_ref, dual_ref, rows_ref,
):
    best, mass, whole = combine(got_ref)
    dual_ref[...] = (jnp.log2(whole) - (best + jnp.log2(mass))) * (EPS / LOG2E)
    speech_total = jnp.sum(row_got_ref[:, 2 * SUB : 3 * SUB, :], axis=0)
    factor = (mass_ref[...] / speech_total) * jnp.exp2(sent_ref[0, 0:SUB, :] - best) / mass
    spread(factor, rows_ref)
    for b in range(SUB):
        carried_ref[:, b * LANES : (b + 1) * LANES] = (
            raw_ref[:, b * LANES : (b + 1) * LANES] * rows_ref[...]
        ).astype(jnp.bfloat16)
    part = 1 - lax.rem(lax.axis_index("row"), 2)
    for p in range(2):
        other_ref[p * 256 : (p + 1) * 256, :] = half_cross(s_ref, part, carried_ref, p).astype(
            jnp.bfloat16
        )


def second_cross_kernel(carried_ref, s_ref, out_ref):
    part = lax.rem(lax.axis_index("row"), 2)
    for p in range(2):
        out_ref[p * 256 : (p + 1) * 256, :] = half_cross(s_ref, part, carried_ref, p)


def pair_kernel(mine_ref, other_ref, out_ref):
    out_ref[...] = (mine_ref[...] + other_ref[...].astype(jnp.float32)).astype(jnp.bfloat16)


def body(speech, speech_mass, text, text_mass):
    rows, width = speech.shape
    columns, row_count = lax.axis_size("col"), lax.axis_size("row")
    cores = 2
    blocks = width // LANES
    big = columns * rows
    flops = 2 * big * big * width

    slices = [text] + [
        lax.ppermute(text, "row", [(i, (i + cores * k) % row_count) for i in range(row_count)])
        for k in range(1, row_count // cores)
    ]
    swap = [(i, i ^ 1) for i in range(row_count)]
    slices = [v for piece in slices for v in (piece, lax.ppermute(piece, "row", swap))]
    piece_rows = blocks * rows + 16
    (x,) = call(
        pack_kernel,
        [bf16(columns, piece_rows, LANES)],
        [
            pltpu.VMEM((rows, width), jnp.bfloat16),
            pltpu.VMEM((1, rows), jnp.float32),
            pltpu.VMEM((piece_rows, LANES), jnp.bfloat16),
            pltpu.SemaphoreType.DMA((2,)),
            pltpu.SemaphoreType.DMA((columns,)),
        ],
        far_args=2,
        far_out=True,
    )(speech, speech_mass.reshape(1, rows))
    x = lax.all_to_all(x, "col", 0, 0)
    column_mass = text_mass.reshape(SUB, LANES)

    scale = LOG2E / (math.sqrt(width) * EPS)
    vector = pltpu.VMEM((SUB, LANES), jnp.float32)
    column = pltpu.VMEM((big, LANES), jnp.float32)
    scores, s, t, row_mass, piece = call(
        lambda *refs: gram_kernel(scale, rows, *refs),
        [
            f32(big, big),
            bf16(blocks, big, LANES),
            bf16(blocks, big, LANES),
            f32(SUB, LANES),
            f32(row_count, 24, LANES),
        ],
        [column, vector, vector, pltpu.SemaphoreType.DMA((row_count,))],
        flops=flops,
        args=1,
        far_args=row_count,
    )(x, *slices)
    row_swap = lambda v: lax.all_to_all(v, "row", 0, 0)
    column_swap = lambda v: lax.all_to_all(v, "col", 0, 0)
    for step in range(ITERS):
        got_row = row_swap(piece)
        if step < ITERS - 1:
            (piece,) = call(row_kernel, [f32(columns, 24, LANES)], args=3)(
                got_row, scores, column_mass
            )
            got = column_swap(piece)
            (piece,) = call(
                column_kernel, [f32(row_count, 24, LANES)], [column, vector, vector], args=3
            )(got, scores, row_mass)
    sent, raw, text_dual = call(
        last_row_kernel,
        [f32(columns, 24, LANES), f32(big, width), f32(SUB, LANES)],
        [pltpu.VMEM((big, big), jnp.bfloat16)],
        flops=flops,
        args=4,
    )(got_row, scores, column_mass, t)
    got = column_swap(sent)
    carried, other, speech_dual = call(
        first_cross_kernel,
        [bf16(big, width), bf16(width // 2, width), f32(SUB, LANES)],
        [column],
        flops=flops // 2,
        args=6,
    )(got, sent, got_row, row_mass, raw, s)
    other = lax.ppermute(other, "row", swap)
    (mine,) = call(second_cross_kernel, [f32(width // 2, width)], flops=flops // 2, args=2)(
        carried, s
    )
    (pair,) = call(pair_kernel, [bf16(width // 2, width)], args=2)(mine, other)
    groups = [
        [r * columns + c for r in range(core, row_count, cores) for c in range(columns)]
        for core in range(cores)
    ]
    count = len(groups[0])
    parts = lax.all_to_all(
        pair.reshape(count, width // 2 // count, width),
        ("row", "col"),
        0,
        0,
        axis_index_groups=groups,
    )
    cross = jnp.sum(parts.astype(jnp.float32), axis=0) * math.sqrt(big * row_count)
    return (cross, speech_dual.reshape(-1), text_dual.reshape(-1))


def solution(mesh):
    return jax.shard_map(
        body,
        mesh=mesh,
        in_specs=(P(("row", "col"), None), P(("row", "col")), P("col", "row"), P("col")),
        out_specs=(P(("row", "col"), None), P("row"), P("col")),
        check_vma=False,
    )
```

```python
import math

import jax
import jax.numpy as jnp
from jax import lax
from jax.experimental import pallas as pl
from jax.experimental.pallas import tpu as pltpu
from jax.sharding import PartitionSpec as P

ITERS = 3
EPS = 0.5
LANES = 128
SUB = 8
LOG2E = math.log2(math.e)
LIMIT = 24 * 1024 * 1024


def call(kernel, outs, scratch=(), flops=0, reads=0, args=0, far_out=False, limit=LIMIT):
    vmem = pl.BlockSpec(memory_space=pltpu.VMEM)
    far = pl.BlockSpec(memory_space=pl.ANY)
    return pl.pallas_call(
        kernel,
        out_shape=outs,
        in_specs=[vmem] * args,
        out_specs=[far if far_out else vmem] * len(outs),
        scratch_shapes=list(scratch),
        compiler_params=pltpu.CompilerParams(vmem_limit_bytes=limit),
        cost_estimate=pl.CostEstimate(flops=flops, bytes_accessed=reads, transcendentals=0),
    )


def f32(*shape):
    return jax.ShapeDtypeStruct(shape, jnp.float32)


def bf16(*shape):
    return jax.ShapeDtypeStruct(shape, jnp.bfloat16)


def total_of(x):
    return jnp.sum(jnp.sum(x, axis=1, keepdims=True), axis=0, keepdims=True)


def combine(got_ref):
    tops = got_ref[:, 0:SUB, :]
    best = jnp.max(tops, axis=0)
    mass = jnp.sum(got_ref[:, SUB : 2 * SUB, :] * jnp.exp2(tops - best[None]), axis=0)
    whole = jnp.sum(got_ref[:, 2 * SUB : 3 * SUB, :], axis=0)
    return best, mass, whole


def send(out_ref, top, mass, whole):
    whole = jnp.broadcast_to(whole, (SUB, LANES))
    for peer in range(out_ref.shape[0]):
        out_ref[peer, 0:SUB, :] = top
        out_ref[peer, SUB : 2 * SUB, :] = mass
        out_ref[peer, 2 * SUB : 3 * SUB, :] = whole


def spread(v, out_ref):
    turned = jnp.concatenate([v, jnp.zeros((LANES - SUB, LANES), jnp.float32)], axis=0).T
    for b in range(SUB):
        out_ref[b * LANES : (b + 1) * LANES, :] = jnp.broadcast_to(
            turned[:, b : b + 1], (LANES, LANES)
        )


def column_stats(scores_ref, rows_ref, top_ref, mass_ref, blocks=range(SUB)):
    for b in blocks:
        values = scores_ref[:, b * LANES : (b + 1) * LANES] + rows_ref[...]
        top = jnp.max(values, axis=0, keepdims=True)
        mass = jnp.sum(jnp.exp2(values - top), axis=0, keepdims=True)
        top_ref[b : b + 1, :] = top
        mass_ref[b : b + 1, :] = mass


def row_stats(scores_ref, v, use=None):
    step = LANES if use is None else 2 * LANES
    lane = lax.broadcasted_iota(jnp.int32, (LANES, LANES), 1)
    shift = jnp.concatenate([v[b : b + 1, :] for b in range(SUB)], axis=1)
    both = jnp.zeros((LANES, LANES), jnp.float32)
    for first in range(0, scores_ref.shape[0], step):
        values = scores_ref[first : first + step, :] + shift
        top = jnp.max(values, axis=1, keepdims=True)
        weights = jnp.exp2(values - top)
        mass = jnp.sum(weights, axis=1, keepdims=True)
        if use is not None:
            use(first, weights)
        for k in range(0, step, LANES):
            b = (first + k) // LANES
            both = jnp.where(lane == b, top[k : k + LANES], both)
            both = jnp.where(lane == SUB + b, mass[k : k + LANES], both)
    turned = both.T
    return turned[0:SUB, :], turned[SUB : 2 * SUB, :]


def pack_kernel(speech_ref, mass_ref, out_ref, piece_ref, sems):
    peers = out_ref.shape[0]
    rows, width = speech_ref.shape
    blocks = width // LANES
    rest = jnp.concatenate([mass_ref[...], mass_ref[...]], axis=1)
    line = lax.broadcasted_iota(jnp.int32, (16, LANES), 0)
    tail = jnp.zeros((16, LANES), jnp.float32)
    for k in range(3):
        term = rest.astype(jnp.bfloat16).astype(jnp.float32)
        tail = jnp.where(line == k, term, tail)
        rest = rest - term
    for lt in range(blocks):
        piece_ref[lt * rows : (lt + 1) * rows, :] = speech_ref[:, lt * LANES : (lt + 1) * LANES]
    piece_ref[blocks * rows :, :] = tail.astype(jnp.bfloat16)
    stores = [pltpu.make_async_copy(piece_ref, out_ref.at[c], sems.at[c]) for c in range(peers)]
    for store in stores:
        store.start()
    for store in stores:
        store.wait()


def place_kernel(*refs):
    slice_refs, t_ref = refs[:-1], refs[-1]
    here = lax.axis_index("row")
    blocks = t_ref.shape[0]
    chips = blocks // 2
    for k in range(blocks):
        t_ref[lax.rem(here // 2 + chips - k // 2, chips) * 2 + lax.rem(here + k, 2)] = slice_refs[k][...]


def unpack_kernel(rows, x_ref, s_ref, turned_ref, mass_ref, column_ref):
    blocks = s_ref.shape[0]
    peers = x_ref.shape[0]
    lane = lax.broadcasted_iota(jnp.int32, (1, LANES), 1)
    base = blocks * rows
    for b in range(SUB):
        pair = []
        for c in (2 * b, 2 * b + 1):
            terms = x_ref[c, base : base + 16, :].astype(jnp.float32)
            pair.append(terms[0:1, :] + terms[1:2, :] + terms[2:3, :])
        mass_ref[b : b + 1, :] = jnp.where(lane < rows, pair[0], pair[1])
    spread(jnp.log2(mass_ref[...]), column_ref)
    for lt in range(blocks):
        for c in range(peers):
            s_ref[lt, c * rows : (c + 1) * rows, :] = x_ref[c, lt * rows : (lt + 1) * rows, :]
        turned_ref[lt] = s_ref[lt].T


def gram_kernel(scale, s_ref, t_ref, mass_ref, column_ref, scores_ref, out_ref, a_ref, b_ref):
    blocks = t_ref.shape[0]
    whole = jnp.concatenate([s_ref[lt] for lt in range(blocks)], axis=1)
    for n in range(4):
        text = jnp.concatenate([t_ref[lt, n * 256 : (n + 1) * 256, :] for lt in range(blocks)], axis=1)
        product = lax.dot_general(
            whole, text, (((1,), (1,)), ((), ())), preferred_element_type=jnp.float32
        )
        scores_ref[:, n * 256 : (n + 1) * 256] = product * scale
        column_stats(scores_ref, column_ref, a_ref, b_ref, (2 * n, 2 * n + 1))
    send(out_ref, a_ref[...], b_ref[...], total_of(mass_ref[...]))


def row_kernel(got_ref, scores_ref, mass_ref, out_ref):
    best, mass, whole = combine(got_ref)
    dual = jnp.log2(whole) - (best + jnp.log2(mass))
    top, mass = row_stats(scores_ref, dual + jnp.log2(mass_ref[...]))
    send(out_ref, top, mass, total_of(mass_ref[...]))


def last_row_kernel(
    got_ref, scores_ref, mass_ref, t_ref, out_ref, raw_ref, dual_ref
):
    best, mass, whole = combine(got_ref)
    dual = jnp.log2(whole) - (best + jnp.log2(mass))
    dual_ref[...] = dual * (EPS / LOG2E)

    text = jnp.concatenate([t_ref[lt] for lt in range(t_ref.shape[0])], axis=1)

    def use(first, weights):
        raw_ref[first : first + weights.shape[0], :] = jnp.dot(
            weights.astype(jnp.bfloat16), text, preferred_element_type=jnp.float32
        )

    top, mass = row_stats(scores_ref, dual + jnp.log2(mass_ref[...]), use)
    send(out_ref, top, mass, total_of(mass_ref[...]))


def column_kernel(got_ref, scores_ref, mass_ref, out_ref, rows_ref, a_ref, b_ref):
    best, mass, whole = combine(got_ref)
    dual = jnp.log2(whole) - (best + jnp.log2(mass))
    spread(dual + jnp.log2(mass_ref[...]), rows_ref)
    column_stats(scores_ref, rows_ref, a_ref, b_ref)
    send(out_ref, a_ref[...], b_ref[...], total_of(mass_ref[...]))


def half_cross(turned_ref, part, carried_ref, p):
    left = jnp.concatenate([turned_ref[4 * p + part], turned_ref[4 * p + 2 + part]], axis=0)
    return jnp.dot(left, carried_ref[...], preferred_element_type=jnp.float32)


def first_cross_kernel(
    got_ref, sent_ref, row_got_ref, mass_ref, raw_ref, turned_ref,
    carried_ref, other_ref, dual_ref, rows_ref,
):
    best, mass, whole = combine(got_ref)
    dual_ref[...] = (jnp.log2(whole) - (best + jnp.log2(mass))) * (EPS / LOG2E)
    speech_total = jnp.sum(row_got_ref[:, 2 * SUB : 3 * SUB, :], axis=0)
    factor = (mass_ref[...] / speech_total) * jnp.exp2(sent_ref[0, 0:SUB, :] - best) / mass
    spread(factor, rows_ref)
    for b in range(SUB):
        carried_ref[:, b * LANES : (b + 1) * LANES] = (
            raw_ref[:, b * LANES : (b + 1) * LANES] * rows_ref[...]
        ).astype(jnp.bfloat16)
    part = 1 - lax.rem(lax.axis_index("row"), 2)
    for p in range(2):
        other_ref[p * 256 : (p + 1) * 256, :] = half_cross(turned_ref, part, carried_ref, p).astype(
            jnp.bfloat16
        )


def second_cross_kernel(carried_ref, turned_ref, out_ref):
    part = lax.rem(lax.axis_index("row"), 2)
    for p in range(2):
        out_ref[p * 256 : (p + 1) * 256, :] = half_cross(turned_ref, part, carried_ref, p)


def pair_kernel(mine_ref, other_ref, out_ref):
    out_ref[...] = (mine_ref[...] + other_ref[...].astype(jnp.float32)).astype(jnp.bfloat16)


def body(speech, speech_mass, text, text_mass):
    rows, width = speech.shape
    columns, row_count = lax.axis_size("col"), lax.axis_size("row")
    cores = 2
    blocks = width // LANES
    big = columns * rows
    flops = 2 * big * big * width

    slices = [text] + [
        lax.ppermute(text, "row", [(i, (i + cores * k) % row_count) for i in range(row_count)])
        for k in range(1, row_count // cores)
    ]
    swap = [(i, i ^ 1) for i in range(row_count)]
    slices = [v for piece in slices for v in (piece, lax.ppermute(piece, "row", swap))]
    piece_rows = blocks * rows + 16
    (x,) = call(
        pack_kernel,
        [bf16(columns, piece_rows, LANES)],
        [
            pltpu.VMEM((piece_rows, LANES), jnp.bfloat16),
            pltpu.SemaphoreType.DMA((columns,)),
        ],
        args=2,
        far_out=True,
        limit=60 * 1024 * 1024,
    )(speech, speech_mass.reshape(1, rows))
    x = lax.all_to_all(x, "col", 0, 0)
    column_mass = text_mass.reshape(SUB, LANES)

    scale = LOG2E / (math.sqrt(width) * EPS)
    vector = pltpu.VMEM((SUB, LANES), jnp.float32)
    column = pltpu.VMEM((big, LANES), jnp.float32)
    (t,) = call(
        place_kernel, [bf16(blocks, big, LANES)], reads=4 * big * width, args=row_count
    )(*slices)
    s, turned, row_mass, row_logs = call(
        lambda *refs: unpack_kernel(rows, *refs),
        [
            bf16(blocks, big, LANES),
            bf16(blocks, LANES, big),
            f32(SUB, LANES),
            f32(big, LANES),
        ],
        args=1,
    )(x)
    scores, piece = call(
        lambda *refs: gram_kernel(scale, *refs),
        [f32(big, big), f32(row_count, 24, LANES)],
        [vector, vector],
        flops=flops,
        args=4,
    )(s, t, row_mass, row_logs)
    row_swap = lambda v: lax.all_to_all(v, "row", 0, 0)
    column_swap = lambda v: lax.all_to_all(v, "col", 0, 0)
    for step in range(ITERS):
        got_row = row_swap(piece)
        if step < ITERS - 1:
            (piece,) = call(row_kernel, [f32(columns, 24, LANES)], args=3)(
                got_row, scores, column_mass
            )
            got = column_swap(piece)
            (piece,) = call(
                column_kernel, [f32(row_count, 24, LANES)], [column, vector, vector], args=3
            )(got, scores, row_mass)
    sent, raw, text_dual = call(
        last_row_kernel,
        [f32(columns, 24, LANES), f32(big, width), f32(SUB, LANES)],
        flops=flops,
        args=4,
    )(got_row, scores, column_mass, t)
    got = column_swap(sent)
    carried, other, speech_dual = call(
        first_cross_kernel,
        [bf16(big, width), bf16(width // 2, width), f32(SUB, LANES)],
        [column],
        flops=flops // 2,
        args=6,
    )(got, sent, got_row, row_mass, raw, turned)
    other = lax.ppermute(other, "row", swap)
    (mine,) = call(second_cross_kernel, [f32(width // 2, width)], flops=flops // 2, args=2)(
        carried, turned
    )
    (pair,) = call(pair_kernel, [bf16(width // 2, width)], args=2)(mine, other)
    groups = [
        [r * columns + c for r in range(core, row_count, cores) for c in range(columns)]
        for core in range(cores)
    ]
    count = len(groups[0])
    parts = lax.all_to_all(
        pair.reshape(count, width // 2 // count, width),
        ("row", "col"),
        0,
        0,
        axis_index_groups=groups,
    )
    cross = jnp.sum(parts.astype(jnp.float32), axis=0) * math.sqrt(big * row_count)
    return (cross, speech_dual.reshape(-1), text_dual.reshape(-1))


def solution(mesh):
    return jax.shard_map(
        body,
        mesh=mesh,
        in_specs=(P(("row", "col"), None), P(("row", "col")), P("col", "row"), P("col")),
        out_specs=(P(("row", "col"), None), P("row"), P("col")),
        check_vma=False,
    )
```

```python
import math

import jax
import jax.numpy as jnp
from jax import lax
from jax.experimental import pallas as pl
from jax.experimental.pallas import tpu as pltpu
from jax.sharding import PartitionSpec as P

ITERS = 3
EPS = 0.5
LANES = 128
SUB = 8
LOG2E = math.log2(math.e)
LIMIT = 24 * 1024 * 1024


def call(kernel, outs, scratch=(), flops=0, reads=0, args=0, far_out=False, limit=LIMIT):
    vmem = pl.BlockSpec(memory_space=pltpu.VMEM)
    far = pl.BlockSpec(memory_space=pl.ANY)
    return pl.pallas_call(
        kernel,
        out_shape=outs,
        in_specs=[vmem] * args,
        out_specs=[far if far_out else vmem] * len(outs),
        scratch_shapes=list(scratch),
        compiler_params=pltpu.CompilerParams(vmem_limit_bytes=limit),
        cost_estimate=pl.CostEstimate(flops=flops, bytes_accessed=reads, transcendentals=0),
    )


def f32(*shape):
    return jax.ShapeDtypeStruct(shape, jnp.float32)


def bf16(*shape):
    return jax.ShapeDtypeStruct(shape, jnp.bfloat16)


def total_of(x):
    return jnp.sum(jnp.sum(x, axis=1, keepdims=True), axis=0, keepdims=True)


def combine(got_ref):
    tops = got_ref[:, 0:SUB, :]
    best = jnp.max(tops, axis=0)
    mass = jnp.sum(got_ref[:, SUB : 2 * SUB, :] * jnp.exp2(tops - best[None]), axis=0)
    whole = jnp.sum(got_ref[:, 2 * SUB : 3 * SUB, :], axis=0)
    return best, mass, whole


def send(out_ref, top, mass, whole):
    whole = jnp.broadcast_to(whole, (SUB, LANES))
    for peer in range(out_ref.shape[0]):
        out_ref[peer, 0:SUB, :] = top
        out_ref[peer, SUB : 2 * SUB, :] = mass
        out_ref[peer, 2 * SUB : 3 * SUB, :] = whole


def spread(v, out_ref):
    turned = jnp.concatenate([v, jnp.zeros((LANES - SUB, LANES), jnp.float32)], axis=0).T
    for b in range(SUB):
        out_ref[b * LANES : (b + 1) * LANES, :] = jnp.broadcast_to(
            turned[:, b : b + 1], (LANES, LANES)
        )


def column_stats(scores_ref, rows_ref, top_ref, mass_ref, held=(), first=0):
    for b in range(first, first + (2 if held else SUB)):
        if held:
            values = held[0][:, (b - first) * LANES : (b - first + 1) * LANES] + rows_ref[...]
        else:
            values = scores_ref[:, b * LANES : (b + 1) * LANES] + rows_ref[...]
        top = jnp.max(values, axis=0, keepdims=True)
        mass = jnp.sum(jnp.exp2(values - top), axis=0, keepdims=True)
        top_ref[b : b + 1, :] = top
        mass_ref[b : b + 1, :] = mass


def row_stats(scores_ref, v, use=None):
    lane = lax.broadcasted_iota(jnp.int32, (LANES, LANES), 1)
    shift = jnp.concatenate([v[b : b + 1, :] for b in range(SUB)], axis=1)
    both = jnp.zeros((LANES, LANES), jnp.float32)
    for b in range(SUB):
        values = scores_ref[b * LANES : (b + 1) * LANES, :] + shift
        top = jnp.max(values, axis=1, keepdims=True)
        weights = jnp.exp2(values - top)
        mass = jnp.sum(weights, axis=1, keepdims=True)
        both = jnp.where(lane == b, top, both)
        both = jnp.where(lane == SUB + b, mass, both)
        if use is not None:
            use(b, weights)
    turned = both.T
    return turned[0:SUB, :], turned[SUB : 2 * SUB, :]


def pack_kernel(speech_ref, mass_ref, out_ref, piece_ref, sems):
    peers = out_ref.shape[0]
    rows, width = speech_ref.shape
    blocks = width // LANES
    rest = jnp.concatenate([mass_ref[...], mass_ref[...]], axis=1)
    line = lax.broadcasted_iota(jnp.int32, (16, LANES), 0)
    tail = jnp.zeros((16, LANES), jnp.float32)
    for k in range(3):
        term = rest.astype(jnp.bfloat16).astype(jnp.float32)
        tail = jnp.where(line == k, term, tail)
        rest = rest - term
    for lt in range(blocks):
        piece_ref[lt * rows : (lt + 1) * rows, :] = speech_ref[:, lt * LANES : (lt + 1) * LANES]
    piece_ref[blocks * rows :, :] = tail.astype(jnp.bfloat16)
    stores = [pltpu.make_async_copy(piece_ref, out_ref.at[c], sems.at[c]) for c in range(peers)]
    for store in stores:
        store.start()
    for store in stores:
        store.wait()


def place_kernel(*refs):
    slice_refs, t_ref = refs[:-1], refs[-1]
    here = lax.axis_index("row")
    blocks = t_ref.shape[0]
    chips = blocks // 2
    for k in range(blocks):
        t_ref[lax.rem(here // 2 + chips - k // 2, chips) * 2 + lax.rem(here + k, 2)] = slice_refs[k][...]


def copy_kernel(piece_ref, out_ref, sems):
    peers = out_ref.shape[0]
    stores = [pltpu.make_async_copy(piece_ref, out_ref.at[c], sems.at[c]) for c in range(peers)]
    for store in stores:
        store.start()
    for store in stores:
        store.wait()


def unpack_kernel(rows, side, x_ref, s_ref, turned_ref, mass_ref, column_ref):
    blocks = s_ref.shape[0]
    peers = x_ref.shape[0]
    core = lax.rem(lax.axis_index("row"), 2)

    def at(c):
        return c + core * ((c % side) * side + c // side - c)

    lane = lax.broadcasted_iota(jnp.int32, (1, LANES), 1)
    base = blocks * rows
    for b in range(SUB):
        pair = []
        for c in (2 * b, 2 * b + 1):
            terms = x_ref[at(c), base : base + 16, :].astype(jnp.float32)
            pair.append(terms[0:1, :] + terms[1:2, :] + terms[2:3, :])
        mass_ref[b : b + 1, :] = jnp.where(lane < rows, pair[0], pair[1])
    spread(jnp.log2(mass_ref[...]), column_ref)
    for lt in range(blocks):
        for c in range(peers):
            s_ref[lt, c * rows : (c + 1) * rows, :] = x_ref[at(c), lt * rows : (lt + 1) * rows, :]
        turned_ref[lt] = s_ref[lt].T


def gram_kernel(scale, s_ref, t_ref, mass_ref, column_ref, scores_ref, out_ref, a_ref, b_ref):
    blocks = t_ref.shape[0]
    whole = jnp.concatenate([s_ref[lt] for lt in range(blocks)], axis=1)
    for n in range(4):
        text = jnp.concatenate([t_ref[lt, n * 256 : (n + 1) * 256, :] for lt in range(blocks)], axis=1)
        product = lax.dot_general(
            whole, text, (((1,), (1,)), ((), ())), preferred_element_type=jnp.float32
        )
        product = product * scale
        scores_ref[:, n * 256 : (n + 1) * 256] = product
        if n > 0:
            column_stats(None, column_ref, a_ref, b_ref, held, 2 * n - 2)
        held = [product]
    column_stats(None, column_ref, a_ref, b_ref, held, 6)
    send(out_ref, a_ref[...], b_ref[...], total_of(mass_ref[...]))


def row_kernel(got_ref, scores_ref, mass_ref, out_ref):
    best, mass, whole = combine(got_ref)
    dual = jnp.log2(whole) - (best + jnp.log2(mass))
    top, mass = row_stats(scores_ref, dual + jnp.log2(mass_ref[...]))
    send(out_ref, top, mass, total_of(mass_ref[...]))


def last_row_kernel(
    got_ref, scores_ref, mass_ref, t_ref, out_ref, raw_ref, dual_ref, *weights_refs
):
    best, mass, whole = combine(got_ref)
    dual = jnp.log2(whole) - (best + jnp.log2(mass))
    dual_ref[...] = dual * (EPS / LOG2E)

    text = jnp.concatenate([t_ref[lt] for lt in range(t_ref.shape[0])], axis=1)


    def product(k):
        raw_ref[k * 256 : (k + 1) * 256, :] = jnp.dot(
            weights_refs[k][...], text, preferred_element_type=jnp.float32
        )

    def use(b, weights):
        rows = slice((b % 2) * LANES, (b % 2 + 1) * LANES)
        weights_refs[b // 2][rows, :] = weights.astype(jnp.bfloat16)
        if b % 2 == 1 and b > 1:
            product(b // 2 - 1)

    top, mass = row_stats(scores_ref, dual + jnp.log2(mass_ref[...]), use)
    product(3)
    send(out_ref, top, mass, total_of(mass_ref[...]))


def column_kernel(got_ref, scores_ref, mass_ref, out_ref, rows_ref, a_ref, b_ref):
    best, mass, whole = combine(got_ref)
    dual = jnp.log2(whole) - (best + jnp.log2(mass))
    spread(dual + jnp.log2(mass_ref[...]), rows_ref)
    column_stats(scores_ref, rows_ref, a_ref, b_ref)
    send(out_ref, a_ref[...], b_ref[...], total_of(mass_ref[...]))


def half_left(turned_ref, part):
    return jnp.concatenate([turned_ref[2 * k + part] for k in range(turned_ref.shape[0] // 2)], axis=0)


def first_cross_kernel(
    got_ref, sent_ref, row_got_ref, mass_ref, raw_ref, turned_ref,
    carried_ref, other_ref, dual_ref, rows_ref,
):
    best, mass, whole = combine(got_ref)
    dual_ref[...] = (jnp.log2(whole) - (best + jnp.log2(mass))) * (EPS / LOG2E)
    speech_total = jnp.sum(row_got_ref[:, 2 * SUB : 3 * SUB, :], axis=0)
    factor = (mass_ref[...] / speech_total) * jnp.exp2(sent_ref[0, 0:SUB, :] - best) / mass
    spread(factor, rows_ref)
    part = 1 - lax.rem(lax.axis_index("row"), 2)
    left = half_left(turned_ref, part)

    def product(n):
        lanes = slice(n * 256, (n + 1) * 256)
        other_ref[:, lanes] = jnp.dot(
            left, carried_ref[:, lanes], preferred_element_type=jnp.float32
        ).astype(jnp.bfloat16)

    for n in range(4):
        for b in (2 * n, 2 * n + 1):
            carried_ref[:, b * LANES : (b + 1) * LANES] = (
                raw_ref[:, b * LANES : (b + 1) * LANES] * rows_ref[...]
            ).astype(jnp.bfloat16)
        if n > 0:
            product(n - 1)
    product(3)


def second_cross_kernel(carried_ref, turned_ref, out_ref):
    left = half_left(turned_ref, lax.rem(lax.axis_index("row"), 2))
    out_ref[...] = jnp.dot(left, carried_ref[...], preferred_element_type=jnp.float32)


def pair_kernel(mine_ref, other_ref, out_ref):
    out_ref[...] = (mine_ref[...] + other_ref[...].astype(jnp.float32)).astype(jnp.bfloat16)


def body(speech, speech_mass, text, text_mass):
    rows, width = speech.shape
    columns, row_count = lax.axis_size("col"), lax.axis_size("row")
    cores = 2
    blocks = width // LANES
    big = columns * rows
    flops = 2 * big * big * width

    slices = [text] + [
        lax.ppermute(text, "row", [(i, (i + cores * k) % row_count) for i in range(row_count)])
        for k in range(1, row_count // cores)
    ]
    swap = [(i, i ^ 1) for i in range(row_count)]
    slices = [v for piece in slices for v in (piece, lax.ppermute(piece, "row", swap))]
    piece_rows = blocks * rows + 16
    side = 4
    along_x = [[x * side + z for x in range(side)] for z in range(side)]
    along_z = [[x * side + z for z in range(side)] for x in range(side)]

    def lines(first, second):
        return [
            [r * columns + c for c in line]
            for r in range(row_count)
            for line in (first if r % cores == 0 else second)
        ]

    (x,) = call(
        pack_kernel,
        [bf16(side, piece_rows, LANES)],
        [
            pltpu.VMEM((piece_rows, LANES), jnp.bfloat16),
            pltpu.SemaphoreType.DMA((side,)),
        ],
        args=2,
        far_out=True,
        limit=60 * 1024 * 1024,
    )(speech, speech_mass.reshape(1, rows))
    x = lax.all_to_all(x, ("row", "col"), 0, 0, axis_index_groups=lines(along_z, along_x))
    (x,) = call(
        copy_kernel,
        [bf16(side, side, piece_rows, LANES)],
        [pltpu.SemaphoreType.DMA((side,))],
        args=1,
        far_out=True,
        limit=60 * 1024 * 1024,
    )(x)
    x = lax.all_to_all(x, ("row", "col"), 0, 0, axis_index_groups=lines(along_x, along_z))
    x = x.reshape(columns, piece_rows, LANES)
    column_mass = text_mass.reshape(SUB, LANES)

    scale = LOG2E / (math.sqrt(width) * EPS)
    vector = pltpu.VMEM((SUB, LANES), jnp.float32)
    column = pltpu.VMEM((big, LANES), jnp.float32)
    (t,) = call(
        place_kernel, [bf16(blocks, big, LANES)], reads=4 * big * width, args=row_count
    )(*slices)
    s, turned, row_mass, row_logs = call(
        lambda *refs: unpack_kernel(rows, side, *refs),
        [
            bf16(blocks, big, LANES),
            bf16(blocks, LANES, big),
            f32(SUB, LANES),
            f32(big, LANES),
        ],
        args=1,
    )(x)
    scores, piece = call(
        lambda *refs: gram_kernel(scale, *refs),
        [f32(big, big), f32(row_count, 24, LANES)],
        [vector, vector],
        flops=flops,
        args=4,
    )(s, t, row_mass, row_logs)
    row_swap = lambda v: lax.all_to_all(v, "row", 0, 0)
    column_swap = lambda v: lax.all_to_all(v, "col", 0, 0)
    for step in range(ITERS):
        got_row = row_swap(piece)
        if step < ITERS - 1:
            (piece,) = call(row_kernel, [f32(columns, 24, LANES)], args=3)(
                got_row, scores, column_mass
            )
            got = column_swap(piece)
            (piece,) = call(
                column_kernel, [f32(row_count, 24, LANES)], [column, vector, vector], args=3
            )(got, scores, row_mass)
    sent, raw, text_dual = call(
        last_row_kernel,
        [f32(columns, 24, LANES), f32(big, width), f32(SUB, LANES)],
        [pltpu.VMEM((big // 4, big), jnp.bfloat16)] * 4,
        flops=flops,
        args=4,
    )(got_row, scores, column_mass, t)
    got = column_swap(sent)
    carried, other, speech_dual = call(
        first_cross_kernel,
        [bf16(big, width), bf16(width // 2, width), f32(SUB, LANES)],
        [column],
        flops=flops // 2,
        args=6,
    )(got, sent, got_row, row_mass, raw, turned)
    other = lax.ppermute(other, "row", swap)
    (mine,) = call(second_cross_kernel, [f32(width // 2, width)], flops=flops // 2, args=2)(
        carried, turned
    )
    (pair,) = call(pair_kernel, [bf16(width // 2, width)], args=2)(mine, other)
    groups = [
        [r * columns + c for r in range(core, row_count, cores) for c in range(columns)]
        for core in range(cores)
    ]
    count = len(groups[0])
    parts = lax.all_to_all(
        pair.reshape(count, width // 2 // count, width),
        ("row", "col"),
        0,
        0,
        axis_index_groups=groups,
    )
    cross = jnp.sum(parts.astype(jnp.float32), axis=0) * math.sqrt(big * row_count)
    return (cross, speech_dual.reshape(-1), text_dual.reshape(-1))


def solution(mesh):
    return jax.shard_map(
        body,
        mesh=mesh,
        in_specs=(P(("row", "col"), None), P(("row", "col")), P("col", "row"), P("col")),
        out_specs=(P(("row", "col"), None), P("row"), P("col")),
        check_vma=False,
    )
```

```python
import math

import jax
import jax.numpy as jnp
from jax import lax
from jax.experimental import pallas as pl
from jax.experimental.pallas import tpu as pltpu
from jax.sharding import PartitionSpec as P

ITERS = 3
EPS = 0.5
LANES = 128
SUB = 8
LOG2E = math.log2(math.e)
LIMIT = 24 * 1024 * 1024


def call(kernel, outs, scratch=(), flops=0, reads=0, args=0):
    vmem = pl.BlockSpec(memory_space=pltpu.VMEM)
    return pl.pallas_call(
        kernel,
        out_shape=outs,
        in_specs=[vmem] * args,
        out_specs=[vmem] * len(outs),
        scratch_shapes=list(scratch),
        compiler_params=pltpu.CompilerParams(vmem_limit_bytes=LIMIT),
        cost_estimate=pl.CostEstimate(flops=flops, bytes_accessed=reads, transcendentals=0),
    )


def f32(*shape):
    return jax.ShapeDtypeStruct(shape, jnp.float32)


def bf16(*shape):
    return jax.ShapeDtypeStruct(shape, jnp.bfloat16)


def total_of(x):
    return jnp.sum(jnp.sum(x, axis=1, keepdims=True), axis=0, keepdims=True)


def combine(got_ref):
    tops = got_ref[:, 0:SUB, :]
    best = jnp.max(tops, axis=0)
    mass = jnp.sum(got_ref[:, SUB : 2 * SUB, :] * jnp.exp2(tops - best[None]), axis=0)
    whole = jnp.sum(got_ref[:, 2 * SUB : 3 * SUB, :], axis=0)
    return best, mass, whole


def send(out_ref, top, mass, whole):
    whole = jnp.broadcast_to(whole, (SUB, LANES))
    for peer in range(out_ref.shape[0]):
        out_ref[peer, 0:SUB, :] = top
        out_ref[peer, SUB : 2 * SUB, :] = mass
        out_ref[peer, 2 * SUB : 3 * SUB, :] = whole


def spread(v, out_ref):
    turned = jnp.concatenate([v, jnp.zeros((LANES - SUB, LANES), jnp.float32)], axis=0).T
    for b in range(SUB):
        out_ref[b * LANES : (b + 1) * LANES, :] = jnp.broadcast_to(
            turned[:, b : b + 1], (LANES, LANES)
        )


def column_stats(scores_ref, rows_ref, top_ref, mass_ref, held=(), first=0):
    for b in range(first, first + (2 if held else SUB)):
        if held:
            values = held[0][:, (b - first) * LANES : (b - first + 1) * LANES] + rows_ref[...]
        else:
            values = scores_ref[:, b * LANES : (b + 1) * LANES] + rows_ref[...]
        top = jnp.max(values, axis=0, keepdims=True)
        mass = jnp.sum(jnp.exp2(values - top), axis=0, keepdims=True)
        top_ref[b : b + 1, :] = top
        mass_ref[b : b + 1, :] = mass


def row_stats(scores_ref, v, use=None):
    lane = lax.broadcasted_iota(jnp.int32, (LANES, LANES), 1)
    shift = jnp.concatenate([v[b : b + 1, :] for b in range(SUB)], axis=1)
    both = jnp.zeros((LANES, LANES), jnp.float32)
    for b in range(SUB):
        values = scores_ref[b * LANES : (b + 1) * LANES, :] + shift
        top = jnp.max(values, axis=1, keepdims=True)
        weights = jnp.exp2(values - top)
        mass = jnp.sum(weights, axis=1, keepdims=True)
        both = jnp.where(lane == b, top, both)
        both = jnp.where(lane == SUB + b, mass, both)
        if use is not None:
            use(b, weights)
    turned = both.T
    return turned[0:SUB, :], turned[SUB : 2 * SUB, :]


def pack_kernel(speech_ref, mass_ref, piece_ref):
    rows, width = speech_ref.shape
    blocks = width // LANES
    rest = jnp.concatenate([mass_ref[...], mass_ref[...]], axis=1)
    line = lax.broadcasted_iota(jnp.int32, (16, LANES), 0)
    tail = jnp.zeros((16, LANES), jnp.float32)
    for k in range(3):
        term = rest.astype(jnp.bfloat16).astype(jnp.float32)
        tail = jnp.where(line == k, term, tail)
        rest = rest - term
    for lt in range(blocks):
        piece_ref[lt * rows : (lt + 1) * rows, :] = speech_ref[:, lt * LANES : (lt + 1) * LANES]
    piece_ref[blocks * rows :, :] = tail.astype(jnp.bfloat16)


def place_kernel(*refs):
    slice_refs, t_ref = refs[:-1], refs[-1]
    here = lax.axis_index("row")
    blocks = t_ref.shape[0]
    chips = blocks // 2
    for k in range(blocks):
        t_ref[lax.rem(here // 2 + chips - k // 2, chips) * 2 + lax.rem(here + k, 2)] = slice_refs[k][...]


def join_kernel(*refs):
    for k, piece_ref in enumerate(refs[:-1]):
        refs[-1][k] = piece_ref[...]


def unpack_kernel(rows, *refs):
    line_refs = refs[:-5]
    s_ref, turned_ref, mass_ref, column_ref, held_ref = refs[-5:]
    side = len(line_refs)
    blocks = s_ref.shape[0]
    core = lax.rem(lax.axis_index("row"), 2)
    here = lax.axis_index("col")
    x, z = here // side, lax.rem(here, side)

    def origin(m, k):
        back_x = m + core * (k - m)
        back_z = k + core * (m - k)
        return lax.rem(x + side - back_x, side) * side + lax.rem(z + side - back_z, side)

    lane = lax.broadcasted_iota(jnp.int32, (1, LANES), 1)
    base = blocks * rows
    for m, line_ref in enumerate(line_refs):
        for k in range(side):
            c = origin(m, k)
            terms = line_ref[k, base : base + 16, :].astype(jnp.float32)
            held_ref[pl.ds(c, 1), :] = terms[0:1, :] + terms[1:2, :] + terms[2:3, :]
            place = pl.ds(pl.multiple_of(c * rows, rows), rows)
            for lt in range(blocks):
                s_ref[lt, place, :] = line_ref[k, lt * rows : (lt + 1) * rows, :]
    for b in range(SUB):
        mass_ref[b : b + 1, :] = jnp.where(
            lane < rows, held_ref[2 * b : 2 * b + 1, :], held_ref[2 * b + 1 : 2 * b + 2, :]
        )
    spread(jnp.log2(mass_ref[...]), column_ref)
    for lt in range(blocks):
        turned_ref[lt] = s_ref[lt].T


def gram_kernel(scale, s_ref, t_ref, mass_ref, column_ref, scores_ref, out_ref, a_ref, b_ref):
    blocks = t_ref.shape[0]
    whole = jnp.concatenate([s_ref[lt] for lt in range(blocks)], axis=1)
    for n in range(4):
        text = jnp.concatenate([t_ref[lt, n * 256 : (n + 1) * 256, :] for lt in range(blocks)], axis=1)
        product = lax.dot_general(
            whole, text, (((1,), (1,)), ((), ())), preferred_element_type=jnp.float32
        )
        product = product * scale
        scores_ref[:, n * 256 : (n + 1) * 256] = product
        if n > 0:
            column_stats(None, column_ref, a_ref, b_ref, held, 2 * n - 2)
        held = [product]
    column_stats(None, column_ref, a_ref, b_ref, held, 6)
    send(out_ref, a_ref[...], b_ref[...], total_of(mass_ref[...]))


def row_kernel(got_ref, scores_ref, mass_ref, out_ref):
    best, mass, whole = combine(got_ref)
    dual = jnp.log2(whole) - (best + jnp.log2(mass))
    top, mass = row_stats(scores_ref, dual + jnp.log2(mass_ref[...]))
    send(out_ref, top, mass, total_of(mass_ref[...]))


def last_row_kernel(
    got_ref, scores_ref, mass_ref, t_ref, out_ref, raw_ref, dual_ref, *weights_refs
):
    best, mass, whole = combine(got_ref)
    dual = jnp.log2(whole) - (best + jnp.log2(mass))
    dual_ref[...] = dual * (EPS / LOG2E)

    text = jnp.concatenate([t_ref[lt] for lt in range(t_ref.shape[0])], axis=1)


    def product(k):
        raw_ref[k * 256 : (k + 1) * 256, :] = jnp.dot(
            weights_refs[k][...], text, preferred_element_type=jnp.float32
        )

    def use(b, weights):
        rows = slice((b % 2) * LANES, (b % 2 + 1) * LANES)
        weights_refs[b // 2][rows, :] = weights.astype(jnp.bfloat16)
        if b % 2 == 1 and b > 1:
            product(b // 2 - 1)

    top, mass = row_stats(scores_ref, dual + jnp.log2(mass_ref[...]), use)
    product(3)
    send(out_ref, top, mass, total_of(mass_ref[...]))


def column_kernel(got_ref, scores_ref, mass_ref, out_ref, rows_ref, a_ref, b_ref):
    best, mass, whole = combine(got_ref)
    dual = jnp.log2(whole) - (best + jnp.log2(mass))
    spread(dual + jnp.log2(mass_ref[...]), rows_ref)
    column_stats(scores_ref, rows_ref, a_ref, b_ref)
    send(out_ref, a_ref[...], b_ref[...], total_of(mass_ref[...]))


def half_left(turned_ref, part):
    return jnp.concatenate([turned_ref[2 * k + part] for k in range(turned_ref.shape[0] // 2)], axis=0)


def first_cross_kernel(
    got_ref, sent_ref, row_got_ref, mass_ref, raw_ref, turned_ref,
    carried_ref, other_ref, dual_ref, rows_ref,
):
    best, mass, whole = combine(got_ref)
    dual_ref[...] = (jnp.log2(whole) - (best + jnp.log2(mass))) * (EPS / LOG2E)
    speech_total = jnp.sum(row_got_ref[:, 2 * SUB : 3 * SUB, :], axis=0)
    factor = (mass_ref[...] / speech_total) * jnp.exp2(sent_ref[0, 0:SUB, :] - best) / mass
    spread(factor, rows_ref)
    part = 1 - lax.rem(lax.axis_index("row"), 2)
    left = half_left(turned_ref, part)

    def product(n):
        lanes = slice(n * 256, (n + 1) * 256)
        other_ref[:, lanes] = jnp.dot(
            left, carried_ref[:, lanes], preferred_element_type=jnp.float32
        ).astype(jnp.bfloat16)

    for n in range(4):
        for b in (2 * n, 2 * n + 1):
            carried_ref[:, b * LANES : (b + 1) * LANES] = (
                raw_ref[:, b * LANES : (b + 1) * LANES] * rows_ref[...]
            ).astype(jnp.bfloat16)
        if n > 0:
            product(n - 1)
    product(3)


def second_cross_kernel(carried_ref, turned_ref, out_ref):
    left = half_left(turned_ref, lax.rem(lax.axis_index("row"), 2))
    out_ref[...] = jnp.dot(left, carried_ref[...], preferred_element_type=jnp.float32)


def pair_kernel(mine_ref, other_ref, out_ref):
    out_ref[...] = (mine_ref[...] + other_ref[...].astype(jnp.float32)).astype(jnp.bfloat16)


def body(speech, speech_mass, text, text_mass):
    rows, width = speech.shape
    columns, row_count = lax.axis_size("col"), lax.axis_size("row")
    cores = 2
    blocks = width // LANES
    big = columns * rows
    flops = 2 * big * big * width

    slices = [text] + [
        lax.ppermute(text, "row", [(i, (i + cores * k) % row_count) for i in range(row_count)])
        for k in range(1, row_count // cores)
    ]
    swap = [(i, i ^ 1) for i in range(row_count)]
    slices = [v for piece in slices for v in (piece, lax.ppermute(piece, "row", swap))]
    piece_rows = blocks * rows + 16
    side = 4

    def shift(v, k, swapped):
        moves = []
        for r in range(row_count):
            for x in range(side):
                for z in range(side):
                    to = (x, (z + k) % side) if r % cores == swapped else ((x + k) % side, z)
                    moves.append((r * columns + x * side + z, r * columns + to[0] * side + to[1]))
        return lax.ppermute(v, ("row", "col"), moves)

    (piece,) = call(pack_kernel, [bf16(piece_rows, LANES)], args=2)(
        speech, speech_mass.reshape(1, rows)
    )
    pieces = [piece] + [shift(piece, k, 0) for k in range(1, side)]
    (line,) = call(join_kernel, [bf16(side, piece_rows, LANES)], args=side)(*pieces)
    lines = [line] + [shift(line, k, 1) for k in range(1, side)]
    column_mass = text_mass.reshape(SUB, LANES)

    scale = LOG2E / (math.sqrt(width) * EPS)
    vector = pltpu.VMEM((SUB, LANES), jnp.float32)
    column = pltpu.VMEM((big, LANES), jnp.float32)
    (t,) = call(
        place_kernel, [bf16(blocks, big, LANES)], reads=4 * big * width, args=row_count
    )(*slices)
    s, turned, row_mass, row_logs = call(
        lambda *refs: unpack_kernel(rows, *refs),
        [
            bf16(blocks, big, LANES),
            bf16(blocks, LANES, big),
            f32(SUB, LANES),
            f32(big, LANES),
        ],
        [pltpu.VMEM((columns, LANES), jnp.float32)],
        args=side,
    )(*lines)
    scores, piece = call(
        lambda *refs: gram_kernel(scale, *refs),
        [f32(big, big), f32(row_count, 24, LANES)],
        [vector, vector],
        flops=flops,
        args=4,
    )(s, t, row_mass, row_logs)
    row_swap = lambda v: lax.all_to_all(v, "row", 0, 0)
    column_swap = lambda v: lax.all_to_all(v, "col", 0, 0)
    for step in range(ITERS):
        got_row = row_swap(piece)
        if step < ITERS - 1:
            (piece,) = call(row_kernel, [f32(columns, 24, LANES)], args=3)(
                got_row, scores, column_mass
            )
            got = column_swap(piece)
            (piece,) = call(
                column_kernel, [f32(row_count, 24, LANES)], [column, vector, vector], args=3
            )(got, scores, row_mass)
    sent, raw, text_dual = call(
        last_row_kernel,
        [f32(columns, 24, LANES), f32(big, width), f32(SUB, LANES)],
        [pltpu.VMEM((big // 4, big), jnp.bfloat16)] * 4,
        flops=flops,
        args=4,
    )(got_row, scores, column_mass, t)
    got = column_swap(sent)
    carried, other, speech_dual = call(
        first_cross_kernel,
        [bf16(big, width), bf16(width // 2, width), f32(SUB, LANES)],
        [column],
        flops=flops // 2,
        args=6,
    )(got, sent, got_row, row_mass, raw, turned)
    other = lax.ppermute(other, "row", swap)
    (mine,) = call(second_cross_kernel, [f32(width // 2, width)], flops=flops // 2, args=2)(
        carried, turned
    )
    (pair,) = call(pair_kernel, [bf16(width // 2, width)], args=2)(mine, other)
    groups = [
        [r * columns + c for r in range(core, row_count, cores) for c in range(columns)]
        for core in range(cores)
    ]
    count = len(groups[0])
    parts = lax.all_to_all(
        pair.reshape(count, width // 2 // count, width),
        ("row", "col"),
        0,
        0,
        axis_index_groups=groups,
    )
    cross = jnp.sum(parts.astype(jnp.float32), axis=0) * math.sqrt(big * row_count)
    return (cross, speech_dual.reshape(-1), text_dual.reshape(-1))


def solution(mesh):
    return jax.shard_map(
        body,
        mesh=mesh,
        in_specs=(P(("row", "col"), None), P(("row", "col")), P("col", "row"), P("col")),
        out_specs=(P(("row", "col"), None), P("row"), P("col")),
        check_vma=False,
    )
```

```python
import functools
import math

import jax
import jax.numpy as jnp
from jax import lax
from jax.experimental import pallas as pl
from jax.experimental.pallas import tpu as pltpu
from jax.sharding import PartitionSpec as P

ITERS = 3
EPS = 0.5
LANES = 128
SUB = 8
LOG2E = math.log2(math.e)
LIMIT = 24 * 1024 * 1024


def call(kernel, outs, scratch=(), flops=0, reads=0, args=0, aliases={}):
    vmem = pl.BlockSpec(memory_space=pltpu.VMEM)
    return pl.pallas_call(
        kernel,
        out_shape=outs,
        in_specs=[vmem] * args,
        out_specs=[vmem] * len(outs),
        scratch_shapes=list(scratch),
        input_output_aliases=aliases,
        compiler_params=pltpu.CompilerParams(vmem_limit_bytes=LIMIT),
        cost_estimate=pl.CostEstimate(flops=flops, bytes_accessed=reads, transcendentals=0),
    )


def f32(*shape):
    return jax.ShapeDtypeStruct(shape, jnp.float32)


def bf16(*shape):
    return jax.ShapeDtypeStruct(shape, jnp.bfloat16)


def total_of(x):
    return jnp.sum(jnp.sum(x, axis=1, keepdims=True), axis=0, keepdims=True)


def combine(got_ref):
    tops = got_ref[:, 0:SUB, :]
    best = jnp.max(tops, axis=0)
    mass = jnp.sum(got_ref[:, SUB : 2 * SUB, :] * jnp.exp2(tops - best[None]), axis=0)
    whole = jnp.sum(got_ref[:, 2 * SUB : 3 * SUB, :], axis=0)
    return best, mass, whole


def send(out_ref, top, mass, whole):
    whole = jnp.broadcast_to(whole, (SUB, LANES))
    for peer in range(out_ref.shape[0]):
        out_ref[peer, 0:SUB, :] = top
        out_ref[peer, SUB : 2 * SUB, :] = mass
        out_ref[peer, 2 * SUB : 3 * SUB, :] = whole


def spread(v, out_ref):
    turned = jnp.concatenate([v, jnp.zeros((LANES - SUB, LANES), jnp.float32)], axis=0).T
    for b in range(SUB):
        out_ref[b * LANES : (b + 1) * LANES, :] = jnp.broadcast_to(
            turned[:, b : b + 1], (LANES, LANES)
        )


def column_stats(scores_ref, rows_ref, top_ref, mass_ref):
    for b in range(SUB):
        values = scores_ref[:, b * LANES : (b + 1) * LANES] + rows_ref[...]
        top = jnp.max(values, axis=0, keepdims=True)
        top_ref[b : b + 1, :] = top
        mass_ref[b : b + 1, :] = jnp.sum(jnp.exp2(values - top), axis=0, keepdims=True)


def row_stats(scores_ref, v, use=None):
    lane = lax.broadcasted_iota(jnp.int32, (LANES, LANES), 1)
    shift = jnp.concatenate([v[b : b + 1, :] for b in range(SUB)], axis=1)
    both = jnp.zeros((LANES, LANES), jnp.float32)
    for b in range(SUB):
        values = scores_ref[b * LANES : (b + 1) * LANES, :] + shift
        top = jnp.max(values, axis=1, keepdims=True)
        weights = jnp.exp2(values - top)
        mass = jnp.sum(weights, axis=1, keepdims=True)
        both = jnp.where(lane == b, top, both)
        both = jnp.where(lane == SUB + b, mass, both)
        if use is not None:
            use(b, weights)
    turned = both.T
    return turned[0:SUB, :], turned[SUB : 2 * SUB, :]


def pack_kernel(speech_ref, mass_ref, piece_ref):
    rows, width = speech_ref.shape
    blocks = width // LANES
    rest = jnp.concatenate([mass_ref[...], mass_ref[...]], axis=1)
    line = lax.broadcasted_iota(jnp.int32, (16, LANES), 0)
    tail = jnp.zeros((16, LANES), jnp.float32)
    for k in range(3):
        term = rest.astype(jnp.bfloat16).astype(jnp.float32)
        tail = jnp.where(line == k, term, tail)
        rest = rest - term
    for lt in range(blocks):
        piece_ref[lt * rows : (lt + 1) * rows, :] = speech_ref[:, lt * LANES : (lt + 1) * LANES]
    piece_ref[blocks * rows :, :] = tail.astype(jnp.bfloat16)


def place_kernel(*refs):
    slice_refs, t_ref = refs[:-1], refs[-1]
    here = lax.axis_index("row")
    blocks = t_ref.shape[0]
    chips = blocks // 2
    for k in range(blocks):
        t_ref[lax.rem(here // 2 + chips - k // 2, chips) * 2 + lax.rem(here + k, 2)] = slice_refs[k][...]


def join_kernel(*refs):
    for k, piece_ref in enumerate(refs[:-1]):
        refs[-1][k] = piece_ref[...]


def lines_kernel(scale, rows, steps, first, last, *refs):
    line_refs, t_ref, refs = refs[: len(steps)], refs[len(steps)], refs[len(steps) + 1 :]
    if first:
        held_ref, stats_ref = None, None
    else:
        held_ref, stats_ref = refs[2:4]
        refs = refs[4:]
    if last:
        scores_ref, s_ref, mass_ref, out_ref, new_held_ref, new_stats_ref, column_ref = refs
    else:
        scores_ref, s_ref, new_held_ref, new_stats_ref, column_ref = refs
    side = line_refs[0].shape[0]
    blocks = t_ref.shape[0]
    core = lax.rem(lax.axis_index("row"), 2)
    here = lax.axis_index("col")
    x, z = here // side, lax.rem(here, side)
    lane = lax.broadcasted_iota(jnp.int32, (1, LANES), 1)
    base = blocks * rows

    def origin(step, k):
        back_x = step + core * (k - step)
        back_z = k + core * (step - k)
        return lax.rem(x + side - back_x, side) * side + lax.rem(z + side - back_z, side)

    pieces = [
        (origin(step, k), line_ref.at[k])
        for step, line_ref in zip(steps, line_refs, strict=True)
        for k in range(side)
    ]
    if not first:
        new_held_ref[...] = held_ref[...]
    masses = []
    for c, piece_ref in pieces:
        terms = piece_ref[base : base + 16, :].astype(jnp.float32)
        masses.append(terms[0:1, :] + terms[1:2, :] + terms[2:3, :])
        new_held_ref[pl.ds(c, 1), :] = masses[-1]
        place = pl.ds(pl.multiple_of(c * rows, rows), rows)
        for lt in range(blocks):
            s_ref[lt, place, :] = piece_ref[lt * rows : (lt + 1) * rows, :]
    empty = jnp.zeros((LANES - len(pieces), LANES), jnp.float32)
    turned = jnp.concatenate([jnp.log2(jnp.concatenate(masses, axis=0)), empty], axis=0).T
    for k in range(len(pieces)):
        column_ref[k * rows : (k + 1) * rows, :] = jnp.broadcast_to(
            turned[0:rows, k : k + 1], (rows, LANES)
        )
    whole = jnp.concatenate(
        [
            jnp.concatenate(
                [piece_ref[lt * rows : (lt + 1) * rows, :] for _, piece_ref in pieces], axis=0
            )
            for lt in range(blocks)
        ],
        axis=1,
    )
    for n in range(4):
        text = jnp.concatenate([t_ref[lt, n * 256 : (n + 1) * 256, :] for lt in range(blocks)], axis=1)
        product = scale * lax.dot_general(
            whole, text, (((1,), (1,)), ((), ())), preferred_element_type=jnp.float32
        )
        for k, (c, _) in enumerate(pieces):
            place = pl.ds(pl.multiple_of(c * rows, rows), rows)
            scores_ref[place, n * 256 : (n + 1) * 256] = product[k * rows : (k + 1) * rows, :]
        for b in (2 * n, 2 * n + 1):
            values = product[:, (b - 2 * n) * LANES : (b - 2 * n + 1) * LANES] + column_ref[...]
            top = jnp.max(values, axis=0, keepdims=True)
            mass = jnp.sum(jnp.exp2(values - top), axis=0, keepdims=True)
            if not first:
                old_top, old_mass = stats_ref[b : b + 1, :], stats_ref[SUB + b : SUB + b + 1, :]
                best = jnp.maximum(top, old_top)
                mass = mass * jnp.exp2(top - best) + old_mass * jnp.exp2(old_top - best)
                top = best
            new_stats_ref[b : b + 1, :] = top
            new_stats_ref[SUB + b : SUB + b + 1, :] = mass
    if last:
        for b in range(SUB):
            mass_ref[b : b + 1, :] = jnp.where(
                lane < rows, new_held_ref[2 * b : 2 * b + 1, :], new_held_ref[2 * b + 1 : 2 * b + 2, :]
            )
        send(out_ref, new_stats_ref[0:SUB, :], new_stats_ref[SUB : 2 * SUB, :], total_of(mass_ref[...]))


def row_kernel(got_ref, scores_ref, mass_ref, out_ref):
    best, mass, whole = combine(got_ref)
    dual = jnp.log2(whole) - (best + jnp.log2(mass))
    top, mass = row_stats(scores_ref, dual + jnp.log2(mass_ref[...]))
    send(out_ref, top, mass, total_of(mass_ref[...]))


def last_row_kernel(
    got_ref, scores_ref, mass_ref, t_ref, out_ref, raw_ref, dual_ref, *weights_refs
):
    best, mass, whole = combine(got_ref)
    dual = jnp.log2(whole) - (best + jnp.log2(mass))
    dual_ref[...] = dual * (EPS / LOG2E)

    text = jnp.concatenate([t_ref[lt] for lt in range(t_ref.shape[0])], axis=1)


    def product(k):
        raw_ref[k * 256 : (k + 1) * 256, :] = jnp.dot(
            weights_refs[k][...], text, preferred_element_type=jnp.float32
        )

    def use(b, weights):
        rows = slice((b % 2) * LANES, (b % 2 + 1) * LANES)
        weights_refs[b // 2][rows, :] = weights.astype(jnp.bfloat16)
        if b % 2 == 1 and b > 1:
            product(b // 2 - 1)

    top, mass = row_stats(scores_ref, dual + jnp.log2(mass_ref[...]), use)
    product(3)
    send(out_ref, top, mass, total_of(mass_ref[...]))


def column_kernel(got_ref, scores_ref, mass_ref, out_ref, rows_ref, a_ref, b_ref):
    best, mass, whole = combine(got_ref)
    dual = jnp.log2(whole) - (best + jnp.log2(mass))
    spread(dual + jnp.log2(mass_ref[...]), rows_ref)
    column_stats(scores_ref, rows_ref, a_ref, b_ref)
    send(out_ref, a_ref[...], b_ref[...], total_of(mass_ref[...]))


def half_cross(s_ref, part, carried):
    left = jnp.concatenate([s_ref[2 * k + part] for k in range(s_ref.shape[0] // 2)], axis=1)
    return lax.dot_general(
        left, carried, (((0,), (0,)), ((), ())), preferred_element_type=jnp.float32
    )


def first_cross_kernel(
    got_ref, sent_ref, row_got_ref, mass_ref, raw_ref, s_ref,
    carried_ref, other_ref, dual_ref, rows_ref,
):
    best, mass, whole = combine(got_ref)
    dual_ref[...] = (jnp.log2(whole) - (best + jnp.log2(mass))) * (EPS / LOG2E)
    speech_total = jnp.sum(row_got_ref[:, 2 * SUB : 3 * SUB, :], axis=0)
    factor = (mass_ref[...] / speech_total) * jnp.exp2(sent_ref[0, 0:SUB, :] - best) / mass
    spread(factor, rows_ref)
    part = 1 - lax.rem(lax.axis_index("row"), 2)

    def product(n):
        lanes = slice(n * 256, (n + 1) * 256)
        other_ref[:, lanes] = half_cross(s_ref, part, carried_ref[:, lanes]).astype(jnp.bfloat16)

    for n in range(4):
        for b in (2 * n, 2 * n + 1):
            carried_ref[:, b * LANES : (b + 1) * LANES] = (
                raw_ref[:, b * LANES : (b + 1) * LANES] * rows_ref[...]
            ).astype(jnp.bfloat16)
        if n > 0:
            product(n - 1)
    product(3)


def second_cross_kernel(carried_ref, s_ref, out_ref):
    out_ref[...] = half_cross(s_ref, lax.rem(lax.axis_index("row"), 2), carried_ref[...])


def pair_kernel(mine_ref, other_ref, out_ref):
    out_ref[...] = (mine_ref[...] + other_ref[...].astype(jnp.float32)).astype(jnp.bfloat16)


def body(speech, speech_mass, text, text_mass):
    rows, width = speech.shape
    columns, row_count = lax.axis_size("col"), lax.axis_size("row")
    cores = 2
    blocks = width // LANES
    big = columns * rows
    flops = 2 * big * big * width

    slices = [text] + [
        lax.ppermute(text, "row", [(i, (i + cores * k) % row_count) for i in range(row_count)])
        for k in range(1, row_count // cores)
    ]
    swap = [(i, i ^ 1) for i in range(row_count)]
    slices = [v for piece in slices for v in (piece, lax.ppermute(piece, "row", swap))]
    piece_rows = blocks * rows + 16
    side = 4

    def shift(v, k, swapped):
        moves = []
        for r in range(row_count):
            for x in range(side):
                for z in range(side):
                    to = (x, (z + k) % side) if r % cores == swapped else ((x + k) % side, z)
                    moves.append((r * columns + x * side + z, r * columns + to[0] * side + to[1]))
        return lax.ppermute(v, ("row", "col"), moves)

    (piece,) = call(pack_kernel, [bf16(piece_rows, LANES)], args=2)(
        speech, speech_mass.reshape(1, rows)
    )
    pieces = [piece] + [shift(piece, k, 0) for k in range(1, side)]
    (line,) = call(join_kernel, [bf16(side, piece_rows, LANES)], args=side)(*pieces)
    lines = [line] + [shift(line, k, 1) for k in range(1, side)]
    column_mass = text_mass.reshape(SUB, LANES)

    scale = LOG2E / (math.sqrt(width) * EPS)
    vector = pltpu.VMEM((SUB, LANES), jnp.float32)
    column = pltpu.VMEM((big, LANES), jnp.float32)
    (t,) = call(
        place_kernel, [bf16(blocks, big, LANES)], args=row_count
    )(*slices)
    grown = [f32(big, big), bf16(blocks, big, LANES)]
    small = [f32(columns, LANES), f32(2 * SUB, LANES)]
    held = call(
        functools.partial(lines_kernel, scale, rows, (0,), True, False),
        grown + small,
        [pltpu.VMEM((big // side, LANES), jnp.float32)],
        args=2,
    )(lines[0], t)
    scores, s, row_mass, piece = call(
        functools.partial(lines_kernel, scale, rows, (1, 2, 3), False, True),
        grown + [f32(SUB, LANES), f32(row_count, 24, LANES)],
        [pltpu.VMEM(v.shape, v.dtype) for v in small]
        + [pltpu.VMEM((big - big // side, LANES), jnp.float32)],
        flops=flops - flops // side,
        args=8,
        aliases={4: 0, 5: 1},
    )(*lines[1:], t, *held)
    row_swap = lambda v: lax.all_to_all(v, "row", 0, 0)
    column_swap = lambda v: lax.all_to_all(v, "col", 0, 0)
    for step in range(ITERS):
        got_row = row_swap(piece)
        if step < ITERS - 1:
            (piece,) = call(row_kernel, [f32(columns, 24, LANES)], args=3)(
                got_row, scores, column_mass
            )
            got = column_swap(piece)
            (piece,) = call(
                column_kernel, [f32(row_count, 24, LANES)], [column, vector, vector], args=3
            )(got, scores, row_mass)
    sent, raw, text_dual = call(
        last_row_kernel,
        [f32(columns, 24, LANES), f32(big, width), f32(SUB, LANES)],
        [pltpu.VMEM((big // 4, big), jnp.bfloat16)] * 4,
        flops=flops,
        args=4,
    )(got_row, scores, column_mass, t)
    got = column_swap(sent)
    carried, other, speech_dual = call(
        first_cross_kernel,
        [bf16(big, width), bf16(width // 2, width), f32(SUB, LANES)],
        [column],
        flops=flops // 2,
        args=6,
    )(got, sent, got_row, row_mass, raw, s)
    other = lax.ppermute(other, "row", swap)
    (mine,) = call(second_cross_kernel, [f32(width // 2, width)], flops=flops // 2, args=2)(
        carried, s
    )
    (pair,) = call(pair_kernel, [bf16(width // 2, width)], args=2)(mine, other)
    groups = [
        [r * columns + c for r in range(core, row_count, cores) for c in range(columns)]
        for core in range(cores)
    ]
    count = len(groups[0])
    parts = lax.all_to_all(
        pair.reshape(count, width // 2 // count, width),
        ("row", "col"),
        0,
        0,
        axis_index_groups=groups,
    )
    cross = jnp.sum(parts.astype(jnp.float32), axis=0) * math.sqrt(big * row_count)
    return (cross, speech_dual.reshape(-1), text_dual.reshape(-1))


def solution(mesh):
    return jax.shard_map(
        body,
        mesh=mesh,
        in_specs=(P(("row", "col"), None), P(("row", "col")), P("col", "row"), P("col")),
        out_specs=(P(("row", "col"), None), P("row"), P("col")),
        check_vma=False,
    )
```

```python
import functools
import math

import jax
import jax.numpy as jnp
from jax import lax
from jax.experimental import pallas as pl
from jax.experimental.pallas import tpu as pltpu
from jax.sharding import PartitionSpec as P

ITERS = 3
EPS = 0.5
LANES = 128
SUB = 8
LOG2E = math.log2(math.e)
LIMIT = 24 * 1024 * 1024


def call(kernel, outs, scratch=(), flops=0, reads=0, args=0, aliases={}):
    vmem = pl.BlockSpec(memory_space=pltpu.VMEM)
    return pl.pallas_call(
        kernel,
        out_shape=outs,
        in_specs=[vmem] * args,
        out_specs=[vmem] * len(outs),
        scratch_shapes=list(scratch),
        input_output_aliases=aliases,
        compiler_params=pltpu.CompilerParams(vmem_limit_bytes=LIMIT),
        cost_estimate=pl.CostEstimate(flops=flops, bytes_accessed=reads, transcendentals=0),
    )


def f32(*shape):
    return jax.ShapeDtypeStruct(shape, jnp.float32)


def bf16(*shape):
    return jax.ShapeDtypeStruct(shape, jnp.bfloat16)


def total_of(x):
    return jnp.sum(jnp.sum(x, axis=1, keepdims=True), axis=0, keepdims=True)


def combine(got_ref):
    tops = got_ref[:, 0:SUB, :]
    best = jnp.max(tops, axis=0)
    mass = jnp.sum(got_ref[:, SUB : 2 * SUB, :] * jnp.exp2(tops - best[None]), axis=0)
    whole = jnp.sum(got_ref[:, 2 * SUB : 3 * SUB, :], axis=0)
    return best, mass, whole


def send(out_ref, top, mass, whole):
    whole = jnp.broadcast_to(whole, (SUB, LANES))
    for peer in range(out_ref.shape[0]):
        out_ref[peer, 0:SUB, :] = top
        out_ref[peer, SUB : 2 * SUB, :] = mass
        out_ref[peer, 2 * SUB : 3 * SUB, :] = whole


def spread(v, out_ref):
    turned = jnp.concatenate([v, jnp.zeros((LANES - SUB, LANES), jnp.float32)], axis=0).T
    for b in range(SUB):
        out_ref[b * LANES : (b + 1) * LANES, :] = jnp.broadcast_to(
            turned[:, b : b + 1], (LANES, LANES)
        )


def column_stats(scores_ref, rows_ref, top_ref, mass_ref):
    for b in range(SUB):
        values = scores_ref[:, b * LANES : (b + 1) * LANES] + rows_ref[...]
        top = jnp.max(values, axis=0, keepdims=True)
        top_ref[b : b + 1, :] = top
        mass_ref[b : b + 1, :] = jnp.sum(jnp.exp2(values - top), axis=0, keepdims=True)


def row_stats(scores_ref, v, use=None):
    lane = lax.broadcasted_iota(jnp.int32, (LANES, LANES), 1)
    shift = jnp.concatenate([v[b : b + 1, :] for b in range(SUB)], axis=1)
    both = jnp.zeros((LANES, LANES), jnp.float32)
    for b in range(SUB):
        values = scores_ref[b * LANES : (b + 1) * LANES, :] + shift
        top = jnp.max(values, axis=1, keepdims=True)
        weights = jnp.exp2(values - top)
        mass = jnp.sum(weights, axis=1, keepdims=True)
        both = jnp.where(lane == b, top, both)
        both = jnp.where(lane == SUB + b, mass, both)
        if use is not None:
            use(b, weights)
    turned = both.T
    return turned[0:SUB, :], turned[SUB : 2 * SUB, :]


def pack_kernel(speech_ref, mass_ref, piece_ref):
    rows, width = speech_ref.shape
    blocks = width // LANES
    rest = jnp.concatenate([mass_ref[...], mass_ref[...]], axis=1)
    line = lax.broadcasted_iota(jnp.int32, (16, LANES), 0)
    tail = jnp.zeros((16, LANES), jnp.float32)
    for k in range(3):
        term = rest.astype(jnp.bfloat16).astype(jnp.float32)
        tail = jnp.where(line == k, term, tail)
        rest = rest - term
    for lt in range(blocks):
        piece_ref[lt * rows : (lt + 1) * rows, :] = speech_ref[:, lt * LANES : (lt + 1) * LANES]
    piece_ref[blocks * rows :, :] = tail.astype(jnp.bfloat16)


def place_kernel(*refs):
    slice_refs, t_ref = refs[:-1], refs[-1]
    here = lax.axis_index("row")
    blocks = t_ref.shape[0]
    chips = blocks // 2
    for k in range(blocks):
        t_ref[lax.rem(here // 2 + chips - k // 2, chips) * 2 + lax.rem(here + k, 2)] = slice_refs[k][...]


def stage_kernel(text_ref, out_ref):
    out_ref[...] = text_ref[...]


def join_kernel(*refs):
    for k, piece_ref in enumerate(refs[:-1]):
        refs[-1][k] = piece_ref[...]


def lines_kernel(scale, rows, steps, first, last, *refs):
    line_refs, t_ref, refs = refs[: len(steps)], refs[len(steps)], refs[len(steps) + 1 :]
    if first:
        held_ref, stats_ref = None, None
    else:
        held_ref, stats_ref = refs[2:4]
        refs = refs[4:]
    if last:
        scores_ref, s_ref, mass_ref, out_ref, new_held_ref, new_stats_ref, column_ref = refs
    else:
        scores_ref, s_ref, new_held_ref, new_stats_ref, column_ref = refs
    side = line_refs[0].shape[0]
    blocks = t_ref.shape[0]
    core = lax.rem(lax.axis_index("row"), 2)
    here = lax.axis_index("col")
    x, z = here // side, lax.rem(here, side)
    lane = lax.broadcasted_iota(jnp.int32, (1, LANES), 1)
    base = blocks * rows

    def origin(step, k):
        back_x = step + core * (k - step)
        back_z = k + core * (step - k)
        return lax.rem(x + side - back_x, side) * side + lax.rem(z + side - back_z, side)

    pieces = [
        (origin(step, k), line_ref.at[k])
        for step, line_ref in zip(steps, line_refs, strict=True)
        for k in range(side)
    ]
    if not first:
        new_held_ref[...] = held_ref[...]
    masses = []
    for c, piece_ref in pieces:
        terms = piece_ref[base : base + 16, :].astype(jnp.float32)
        masses.append(terms[0:1, :] + terms[1:2, :] + terms[2:3, :])
        new_held_ref[pl.ds(c, 1), :] = masses[-1]
        place = pl.ds(pl.multiple_of(c * rows, rows), rows)
        for lt in range(blocks):
            s_ref[lt, place, :] = piece_ref[lt * rows : (lt + 1) * rows, :]
    empty = jnp.zeros((LANES - len(pieces), LANES), jnp.float32)
    turned = jnp.concatenate([jnp.log2(jnp.concatenate(masses, axis=0)), empty], axis=0).T
    for k in range(len(pieces)):
        column_ref[k * rows : (k + 1) * rows, :] = jnp.broadcast_to(
            turned[0:rows, k : k + 1], (rows, LANES)
        )
    whole = jnp.concatenate(
        [
            jnp.concatenate(
                [piece_ref[lt * rows : (lt + 1) * rows, :] for _, piece_ref in pieces], axis=0
            )
            for lt in range(blocks)
        ],
        axis=1,
    )
    for n in range(4):
        text = jnp.concatenate([t_ref[lt, n * 256 : (n + 1) * 256, :] for lt in range(blocks)], axis=1)
        product = scale * lax.dot_general(
            whole, text, (((1,), (1,)), ((), ())), preferred_element_type=jnp.float32
        )
        for k, (c, _) in enumerate(pieces):
            place = pl.ds(pl.multiple_of(c * rows, rows), rows)
            scores_ref[place, n * 256 : (n + 1) * 256] = product[k * rows : (k + 1) * rows, :]
        for b in (2 * n, 2 * n + 1):
            values = product[:, (b - 2 * n) * LANES : (b - 2 * n + 1) * LANES] + column_ref[...]
            top = jnp.max(values, axis=0, keepdims=True)
            mass = jnp.sum(jnp.exp2(values - top), axis=0, keepdims=True)
            if not first:
                old_top, old_mass = stats_ref[b : b + 1, :], stats_ref[SUB + b : SUB + b + 1, :]
                best = jnp.maximum(top, old_top)
                mass = mass * jnp.exp2(top - best) + old_mass * jnp.exp2(old_top - best)
                top = best
            new_stats_ref[b : b + 1, :] = top
            new_stats_ref[SUB + b : SUB + b + 1, :] = mass
    if last:
        for b in range(SUB):
            mass_ref[b : b + 1, :] = jnp.where(
                lane < rows, new_held_ref[2 * b : 2 * b + 1, :], new_held_ref[2 * b + 1 : 2 * b + 2, :]
            )
        send(out_ref, new_stats_ref[0:SUB, :], new_stats_ref[SUB : 2 * SUB, :], total_of(mass_ref[...]))


def row_kernel(got_ref, scores_ref, mass_ref, out_ref):
    best, mass, whole = combine(got_ref)
    dual = jnp.log2(whole) - (best + jnp.log2(mass))
    top, mass = row_stats(scores_ref, dual + jnp.log2(mass_ref[...]))
    send(out_ref, top, mass, total_of(mass_ref[...]))


def last_row_kernel(
    got_ref, scores_ref, mass_ref, t_ref, out_ref, raw_ref, dual_ref, *weights_refs
):
    best, mass, whole = combine(got_ref)
    dual = jnp.log2(whole) - (best + jnp.log2(mass))
    dual_ref[...] = dual * (EPS / LOG2E)

    text = jnp.concatenate([t_ref[lt] for lt in range(t_ref.shape[0])], axis=1)


    def product(k):
        raw_ref[k * 256 : (k + 1) * 256, :] = jnp.dot(
            weights_refs[k][...], text, preferred_element_type=jnp.float32
        )

    def use(b, weights):
        rows = slice((b % 2) * LANES, (b % 2 + 1) * LANES)
        weights_refs[b // 2][rows, :] = weights.astype(jnp.bfloat16)
        if b % 2 == 1 and b > 1:
            product(b // 2 - 1)

    top, mass = row_stats(scores_ref, dual + jnp.log2(mass_ref[...]), use)
    product(3)
    send(out_ref, top, mass, total_of(mass_ref[...]))


def column_kernel(got_ref, scores_ref, mass_ref, out_ref, rows_ref, a_ref, b_ref):
    best, mass, whole = combine(got_ref)
    dual = jnp.log2(whole) - (best + jnp.log2(mass))
    spread(dual + jnp.log2(mass_ref[...]), rows_ref)
    column_stats(scores_ref, rows_ref, a_ref, b_ref)
    send(out_ref, a_ref[...], b_ref[...], total_of(mass_ref[...]))


def half_cross(s_ref, part, carried):
    left = jnp.concatenate([s_ref[2 * k + part] for k in range(s_ref.shape[0] // 2)], axis=1)
    return lax.dot_general(
        left, carried, (((0,), (0,)), ((), ())), preferred_element_type=jnp.float32
    )


def first_cross_kernel(
    got_ref, sent_ref, row_got_ref, mass_ref, raw_ref, s_ref,
    carried_ref, other_ref, dual_ref, rows_ref,
):
    best, mass, whole = combine(got_ref)
    dual_ref[...] = (jnp.log2(whole) - (best + jnp.log2(mass))) * (EPS / LOG2E)
    speech_total = jnp.sum(row_got_ref[:, 2 * SUB : 3 * SUB, :], axis=0)
    factor = (mass_ref[...] / speech_total) * jnp.exp2(sent_ref[0, 0:SUB, :] - best) / mass
    spread(factor, rows_ref)
    part = 1 - lax.rem(lax.axis_index("row"), 2)

    def product(n):
        lanes = slice(n * 256, (n + 1) * 256)
        other_ref[:, lanes] = half_cross(s_ref, part, carried_ref[:, lanes]).astype(jnp.bfloat16)

    for n in range(4):
        for b in (2 * n, 2 * n + 1):
            carried_ref[:, b * LANES : (b + 1) * LANES] = (
                raw_ref[:, b * LANES : (b + 1) * LANES] * rows_ref[...]
            ).astype(jnp.bfloat16)
        if n > 0:
            product(n - 1)
    product(3)


def second_cross_kernel(carried_ref, s_ref, out_ref):
    out_ref[...] = half_cross(s_ref, lax.rem(lax.axis_index("row"), 2), carried_ref[...])


def pair_kernel(mine_ref, other_ref, out_ref):
    out_ref[...] = (mine_ref[...] + other_ref[...].astype(jnp.float32)).astype(jnp.bfloat16)


def body(speech, speech_mass, text, text_mass):
    rows, width = speech.shape
    columns, row_count = lax.axis_size("col"), lax.axis_size("row")
    cores = 2
    blocks = width // LANES
    big = columns * rows
    flops = 2 * big * big * width

    swap = [(i, i ^ 1) for i in range(row_count)]

    def back(v, k):
        return lax.ppermute(v, "row", [(i, (i + cores * k) % row_count) for i in range(row_count)])

    piece_rows = blocks * rows + 16
    side = 4

    def shift(v, k, swapped):
        moves = []
        for r in range(row_count):
            for x in range(side):
                for z in range(side):
                    to = (x, (z + k) % side) if r % cores == swapped else ((x + k) % side, z)
                    moves.append((r * columns + x * side + z, r * columns + to[0] * side + to[1]))
        return lax.ppermute(v, ("row", "col"), moves)

    (piece,) = call(pack_kernel, [bf16(piece_rows, LANES)], args=2)(
        speech, speech_mass.reshape(1, rows)
    )
    pieces = [piece] + [shift(piece, k, 0) for k in range(1, side)]
    beside = back(text, 1), back(text, 3)
    (line,) = call(join_kernel, [bf16(side, piece_rows, LANES)], args=side)(*pieces)
    late, line = lax.optimization_barrier((text, line))
    lines = [line] + [shift(line, k, 1) for k in range(1, side)]
    (own,) = call(stage_kernel, [bf16(*text.shape)], args=1)(late)
    slices = [own, beside[0], back(late, 2), beside[1]]
    slices = [v for piece in slices for v in (piece, lax.ppermute(piece, "row", swap))]
    column_mass = text_mass.reshape(SUB, LANES)

    scale = LOG2E / (math.sqrt(width) * EPS)
    vector = pltpu.VMEM((SUB, LANES), jnp.float32)
    column = pltpu.VMEM((big, LANES), jnp.float32)
    (t,) = call(
        place_kernel, [bf16(blocks, big, LANES)], args=row_count
    )(*slices)
    grown = [f32(big, big), bf16(blocks, big, LANES)]
    small = [f32(columns, LANES), f32(2 * SUB, LANES)]
    held = call(
        functools.partial(lines_kernel, scale, rows, (0,), True, False),
        grown + small,
        [pltpu.VMEM((big // side, LANES), jnp.float32)],
        args=2,
    )(lines[0], t)
    scores, s, row_mass, piece = call(
        functools.partial(lines_kernel, scale, rows, (1, 2, 3), False, True),
        grown + [f32(SUB, LANES), f32(row_count, 24, LANES)],
        [pltpu.VMEM(v.shape, v.dtype) for v in small]
        + [pltpu.VMEM((big - big // side, LANES), jnp.float32)],
        flops=flops - flops // side,
        args=8,
        aliases={4: 0, 5: 1},
    )(*lines[1:], t, *held)
    row_swap = lambda v: lax.all_to_all(v, "row", 0, 0)
    column_swap = lambda v: lax.all_to_all(v, "col", 0, 0)
    for step in range(ITERS):
        got_row = row_swap(piece)
        if step < ITERS - 1:
            (piece,) = call(row_kernel, [f32(columns, 24, LANES)], args=3)(
                got_row, scores, column_mass
            )
            got = column_swap(piece)
            (piece,) = call(
                column_kernel, [f32(row_count, 24, LANES)], [column, vector, vector], args=3
            )(got, scores, row_mass)
    sent, raw, text_dual = call(
        last_row_kernel,
        [f32(columns, 24, LANES), f32(big, width), f32(SUB, LANES)],
        [pltpu.VMEM((big // 4, big), jnp.bfloat16)] * 4,
        flops=flops,
        args=4,
    )(got_row, scores, column_mass, t)
    got = column_swap(sent)
    carried, other, speech_dual = call(
        first_cross_kernel,
        [bf16(big, width), bf16(width // 2, width), f32(SUB, LANES)],
        [column],
        flops=flops // 2,
        args=6,
    )(got, sent, got_row, row_mass, raw, s)
    other = lax.ppermute(other, "row", swap)
    (mine,) = call(second_cross_kernel, [f32(width // 2, width)], flops=flops // 2, args=2)(
        carried, s
    )
    (pair,) = call(pair_kernel, [bf16(width // 2, width)], args=2)(mine, other)
    groups = [
        [r * columns + c for r in range(core, row_count, cores) for c in range(columns)]
        for core in range(cores)
    ]
    count = len(groups[0])
    parts = lax.all_to_all(
        pair.reshape(count, width // 2 // count, width),
        ("row", "col"),
        0,
        0,
        axis_index_groups=groups,
    )
    cross = jnp.sum(parts.astype(jnp.float32), axis=0) * math.sqrt(big * row_count)
    return (cross, speech_dual.reshape(-1), text_dual.reshape(-1))


def solution(mesh):
    return jax.shard_map(
        body,
        mesh=mesh,
        in_specs=(P(("row", "col"), None), P(("row", "col")), P("col", "row"), P("col")),
        out_specs=(P(("row", "col"), None), P("row"), P("col")),
        check_vma=False,
    )
```

```python
import functools
import math

import jax
import jax.numpy as jnp
from jax import lax
from jax.experimental import pallas as pl
from jax.experimental.pallas import tpu as pltpu
from jax.sharding import PartitionSpec as P

ITERS = 3
EPS = 0.5
LANES = 128
SUB = 8
LOG2E = math.log2(math.e)
LIMIT = 24 * 1024 * 1024


def call(kernel, outs, scratch=(), flops=0, reads=0, args=0, aliases={}):
    vmem = pl.BlockSpec(memory_space=pltpu.VMEM)
    return pl.pallas_call(
        kernel,
        out_shape=outs,
        in_specs=[vmem] * args,
        out_specs=[vmem] * len(outs),
        scratch_shapes=list(scratch),
        input_output_aliases=aliases,
        compiler_params=pltpu.CompilerParams(vmem_limit_bytes=LIMIT),
        cost_estimate=pl.CostEstimate(flops=flops, bytes_accessed=reads, transcendentals=0),
    )


def f32(*shape):
    return jax.ShapeDtypeStruct(shape, jnp.float32)


def bf16(*shape):
    return jax.ShapeDtypeStruct(shape, jnp.bfloat16)


def total_of(x):
    return jnp.sum(jnp.sum(x, axis=1, keepdims=True), axis=0, keepdims=True)


def combine(got_ref):
    tops = got_ref[:, 0:SUB, :]
    best = jnp.max(tops, axis=0)
    mass = jnp.sum(got_ref[:, SUB : 2 * SUB, :] * jnp.exp2(tops - best[None]), axis=0)
    whole = jnp.sum(got_ref[:, 2 * SUB : 3 * SUB, :], axis=0)
    return best, mass, whole


def send(out_ref, top, mass, whole):
    whole = jnp.broadcast_to(whole, (SUB, LANES))
    for peer in range(out_ref.shape[0]):
        out_ref[peer, 0:SUB, :] = top
        out_ref[peer, SUB : 2 * SUB, :] = mass
        out_ref[peer, 2 * SUB : 3 * SUB, :] = whole


def spread(v, out_ref):
    turned = jnp.concatenate([v, jnp.zeros((LANES - SUB, LANES), jnp.float32)], axis=0).T
    for b in range(SUB):
        out_ref[b * LANES : (b + 1) * LANES, :] = jnp.broadcast_to(
            turned[:, b : b + 1], (LANES, LANES)
        )


def column_stats(scores_ref, rows_ref, top_ref, mass_ref):
    for b in range(SUB):
        values = scores_ref[:, b * LANES : (b + 1) * LANES] + rows_ref[...]
        top = jnp.max(values, axis=0, keepdims=True)
        top_ref[b : b + 1, :] = top
        mass_ref[b : b + 1, :] = jnp.sum(jnp.exp2(values - top), axis=0, keepdims=True)


def row_stats(scores_ref, v, use=None):
    lane = lax.broadcasted_iota(jnp.int32, (LANES, LANES), 1)
    shift = jnp.concatenate([v[b : b + 1, :] for b in range(SUB)], axis=1)
    both = jnp.zeros((LANES, LANES), jnp.float32)
    for b in range(SUB):
        values = scores_ref[b * LANES : (b + 1) * LANES, :] + shift
        top = jnp.max(values, axis=1, keepdims=True)
        weights = jnp.exp2(values - top)
        mass = jnp.sum(weights, axis=1, keepdims=True)
        both = jnp.where(lane == b, top, both)
        both = jnp.where(lane == SUB + b, mass, both)
        if use is not None:
            use(b, weights)
    turned = both.T
    return turned[0:SUB, :], turned[SUB : 2 * SUB, :]


def pack_kernel(speech_ref, mass_ref, piece_ref):
    rows, width = speech_ref.shape
    blocks = width // LANES
    rest = jnp.concatenate([mass_ref[...], mass_ref[...]], axis=1)
    line = lax.broadcasted_iota(jnp.int32, (16, LANES), 0)
    tail = jnp.zeros((16, LANES), jnp.float32)
    for k in range(3):
        term = rest.astype(jnp.bfloat16).astype(jnp.float32)
        tail = jnp.where(line == k, term, tail)
        rest = rest - term
    for lt in range(blocks):
        piece_ref[lt * rows : (lt + 1) * rows, :] = speech_ref[:, lt * LANES : (lt + 1) * LANES]
    piece_ref[blocks * rows :, :] = tail.astype(jnp.bfloat16)


def place_kernel(*refs):
    slice_refs, t_ref = refs[:-1], refs[-1]
    here = lax.axis_index("row")
    blocks = t_ref.shape[0]
    chips = blocks // 2
    for k in range(blocks):
        t_ref[lax.rem(here // 2 + chips - k // 2, chips) * 2 + lax.rem(here + k, 2)] = slice_refs[k][...]


def join_kernel(*refs):
    for k, piece_ref in enumerate(refs[:-1]):
        refs[-1][k] = piece_ref[...]


def lines_kernel(scale, rows, steps, first, last, *refs):
    line_refs, t_ref, refs = refs[: len(steps)], refs[len(steps)], refs[len(steps) + 1 :]
    if first:
        held_ref, stats_ref = None, None
    else:
        held_ref, stats_ref = refs[2:4]
        refs = refs[4:]
    if last:
        scores_ref, s_ref, mass_ref, out_ref, new_held_ref, new_stats_ref, column_ref = refs
    else:
        scores_ref, s_ref, new_held_ref, new_stats_ref, column_ref = refs
    side = line_refs[0].shape[0]
    blocks = t_ref.shape[0]
    core = lax.rem(lax.axis_index("row"), 2)
    here = lax.axis_index("col")
    x, z = here // side, lax.rem(here, side)
    lane = lax.broadcasted_iota(jnp.int32, (1, LANES), 1)
    base = blocks * rows

    def origin(step, k):
        back_x = step + core * (k - step)
        back_z = k + core * (step - k)
        return lax.rem(x + side - back_x, side) * side + lax.rem(z + side - back_z, side)

    pieces = [
        (origin(step, k), line_ref.at[k])
        for step, line_ref in zip(steps, line_refs, strict=True)
        for k in range(side)
    ]
    if not first:
        new_held_ref[...] = held_ref[...]
    masses = []
    for c, piece_ref in pieces:
        terms = piece_ref[base : base + 16, :].astype(jnp.float32)
        masses.append(terms[0:1, :] + terms[1:2, :] + terms[2:3, :])
        new_held_ref[pl.ds(c, 1), :] = masses[-1]
        place = pl.ds(pl.multiple_of(c * rows, rows), rows)
        for lt in range(blocks):
            s_ref[lt, place, :] = piece_ref[lt * rows : (lt + 1) * rows, :]
    empty = jnp.zeros((LANES - len(pieces), LANES), jnp.float32)
    turned = jnp.concatenate([jnp.log2(jnp.concatenate(masses, axis=0)), empty], axis=0).T
    for k in range(len(pieces)):
        column_ref[k * rows : (k + 1) * rows, :] = jnp.broadcast_to(
            turned[0:rows, k : k + 1], (rows, LANES)
        )
    whole = jnp.concatenate(
        [
            jnp.concatenate(
                [piece_ref[lt * rows : (lt + 1) * rows, :] for _, piece_ref in pieces], axis=0
            )
            for lt in range(blocks)
        ],
        axis=1,
    )
    for n in range(4):
        text = jnp.concatenate([t_ref[lt, n * 256 : (n + 1) * 256, :] for lt in range(blocks)], axis=1)
        product = scale * lax.dot_general(
            whole, text, (((1,), (1,)), ((), ())), preferred_element_type=jnp.float32
        )
        for k, (c, _) in enumerate(pieces):
            place = pl.ds(pl.multiple_of(c * rows, rows), rows)
            scores_ref[place, n * 256 : (n + 1) * 256] = product[k * rows : (k + 1) * rows, :]
        for b in (2 * n, 2 * n + 1):
            values = product[:, (b - 2 * n) * LANES : (b - 2 * n + 1) * LANES] + column_ref[...]
            top = jnp.max(values, axis=0, keepdims=True)
            mass = jnp.sum(jnp.exp2(values - top), axis=0, keepdims=True)
            if not first:
                old_top, old_mass = stats_ref[b : b + 1, :], stats_ref[SUB + b : SUB + b + 1, :]
                best = jnp.maximum(top, old_top)
                mass = mass * jnp.exp2(top - best) + old_mass * jnp.exp2(old_top - best)
                top = best
            new_stats_ref[b : b + 1, :] = top
            new_stats_ref[SUB + b : SUB + b + 1, :] = mass
    if last:
        for b in range(SUB):
            mass_ref[b : b + 1, :] = jnp.where(
                lane < rows, new_held_ref[2 * b : 2 * b + 1, :], new_held_ref[2 * b + 1 : 2 * b + 2, :]
            )
        send(out_ref, new_stats_ref[0:SUB, :], new_stats_ref[SUB : 2 * SUB, :], total_of(mass_ref[...]))


def row_kernel(got_ref, scores_ref, mass_ref, out_ref):
    best, mass, whole = combine(got_ref)
    dual = jnp.log2(whole) - (best + jnp.log2(mass))
    top, mass = row_stats(scores_ref, dual + jnp.log2(mass_ref[...]))
    send(out_ref, top, mass, total_of(mass_ref[...]))


def last_row_kernel(
    got_ref, scores_ref, mass_ref, t_ref, out_ref, raw_ref, dual_ref, *weights_refs
):
    best, mass, whole = combine(got_ref)
    dual = jnp.log2(whole) - (best + jnp.log2(mass))
    dual_ref[...] = dual * (EPS / LOG2E)

    text = jnp.concatenate([t_ref[lt] for lt in range(t_ref.shape[0])], axis=1)


    def product(k):
        raw_ref[k * 256 : (k + 1) * 256, :] = jnp.dot(
            weights_refs[k][...], text, preferred_element_type=jnp.float32
        )

    def use(b, weights):
        rows = slice((b % 2) * LANES, (b % 2 + 1) * LANES)
        weights_refs[b // 2][rows, :] = weights.astype(jnp.bfloat16)
        if b % 2 == 1 and b > 1:
            product(b // 2 - 1)

    top, mass = row_stats(scores_ref, dual + jnp.log2(mass_ref[...]), use)
    product(3)
    send(out_ref, top, mass, total_of(mass_ref[...]))


def column_kernel(got_ref, scores_ref, mass_ref, out_ref, rows_ref, a_ref, b_ref):
    best, mass, whole = combine(got_ref)
    dual = jnp.log2(whole) - (best + jnp.log2(mass))
    spread(dual + jnp.log2(mass_ref[...]), rows_ref)
    column_stats(scores_ref, rows_ref, a_ref, b_ref)
    send(out_ref, a_ref[...], b_ref[...], total_of(mass_ref[...]))


def half_cross(s_ref, part, carried):
    left = jnp.concatenate([s_ref[2 * k + part] for k in range(s_ref.shape[0] // 2)], axis=1)
    return lax.dot_general(
        left, carried, (((0,), (0,)), ((), ())), preferred_element_type=jnp.float32
    )


def first_cross_kernel(
    got_ref, sent_ref, row_got_ref, mass_ref, raw_ref, s_ref,
    carried_ref, other_ref, dual_ref, rows_ref,
):
    best, mass, whole = combine(got_ref)
    dual_ref[...] = (jnp.log2(whole) - (best + jnp.log2(mass))) * (EPS / LOG2E)
    speech_total = jnp.sum(row_got_ref[:, 2 * SUB : 3 * SUB, :], axis=0)
    factor = (mass_ref[...] / speech_total) * jnp.exp2(sent_ref[0, 0:SUB, :] - best) / mass
    spread(factor, rows_ref)
    part = 1 - lax.rem(lax.axis_index("row"), 2)

    def product(n):
        lanes = slice(n * 256, (n + 1) * 256)
        other_ref[:, lanes] = half_cross(s_ref, part, carried_ref[:, lanes]).astype(jnp.bfloat16)

    for n in range(4):
        for b in (2 * n, 2 * n + 1):
            carried_ref[:, b * LANES : (b + 1) * LANES] = (
                raw_ref[:, b * LANES : (b + 1) * LANES] * rows_ref[...]
            ).astype(jnp.bfloat16)
        if n > 0:
            product(n - 1)
    product(3)


def second_cross_kernel(carried_ref, s_ref, out_ref):
    out_ref[...] = half_cross(s_ref, lax.rem(lax.axis_index("row"), 2), carried_ref[...])


def pair_kernel(mine_ref, other_ref, out_ref):
    out_ref[...] = (mine_ref[...] + other_ref[...].astype(jnp.float32)).astype(jnp.bfloat16)


def body(speech, speech_mass, text, text_mass):
    rows, width = speech.shape
    columns, row_count = lax.axis_size("col"), lax.axis_size("row")
    cores = 2
    blocks = width // LANES
    big = columns * rows
    flops = 2 * big * big * width

    swap = [(i, i ^ 1) for i in range(row_count)]

    def back(v, k):
        return lax.ppermute(v, "row", [(i, (i + cores * k) % row_count) for i in range(row_count)])

    piece_rows = blocks * rows + 16
    side = 4

    def shift(v, k, swapped):
        moves = []
        for r in range(row_count):
            for x in range(side):
                for z in range(side):
                    to = (x, (z + k) % side) if r % cores == swapped else ((x + k) % side, z)
                    moves.append((r * columns + x * side + z, r * columns + to[0] * side + to[1]))
        return lax.ppermute(v, ("row", "col"), moves)

    (piece,) = call(pack_kernel, [bf16(piece_rows, LANES)], args=2)(
        speech, speech_mass.reshape(1, rows)
    )
    pieces = [piece] + [shift(piece, k, 0) for k in range(1, side)]
    beside = back(text, 1), back(text, 3)
    (line,) = call(join_kernel, [bf16(side, piece_rows, LANES)], args=side)(*pieces)
    late, line = lax.optimization_barrier((text, line))
    lines = [line] + [shift(line, k, 1) for k in range(1, side)]
    slices = [late, beside[0], back(late, 2), beside[1]]
    slices = [v for piece in slices for v in (piece, lax.ppermute(piece, "row", swap))]
    column_mass = text_mass.reshape(SUB, LANES)

    scale = LOG2E / (math.sqrt(width) * EPS)
    vector = pltpu.VMEM((SUB, LANES), jnp.float32)
    column = pltpu.VMEM((big, LANES), jnp.float32)
    (t,) = call(
        place_kernel, [bf16(blocks, big, LANES)], args=row_count
    )(*slices)
    grown = [f32(big, big), bf16(blocks, big, LANES)]
    small = [f32(columns, LANES), f32(2 * SUB, LANES)]
    held = call(
        functools.partial(lines_kernel, scale, rows, (0,), True, False),
        grown + small,
        [pltpu.VMEM((big // side, LANES), jnp.float32)],
        args=2,
    )(lines[0], t)
    held = call(
        functools.partial(lines_kernel, scale, rows, (1, 3), False, False),
        grown + small,
        [pltpu.VMEM((big // 2, LANES), jnp.float32)],
        args=7,
        aliases={3: 0, 4: 1},
    )(lines[1], lines[3], t, *held)
    scores, s, row_mass, piece = call(
        functools.partial(lines_kernel, scale, rows, (2,), False, True),
        grown + [f32(SUB, LANES), f32(row_count, 24, LANES)],
        [pltpu.VMEM(v.shape, v.dtype) for v in small]
        + [pltpu.VMEM((big // side, LANES), jnp.float32)],
        flops=flops // side,
        args=6,
        aliases={2: 0, 3: 1},
    )(lines[2], t, *held)
    row_swap = lambda v: lax.all_to_all(v, "row", 0, 0)
    column_swap = lambda v: lax.all_to_all(v, "col", 0, 0)
    for step in range(ITERS):
        got_row = row_swap(piece)
        if step < ITERS - 1:
            (piece,) = call(row_kernel, [f32(columns, 24, LANES)], args=3)(
                got_row, scores, column_mass
            )
            got = column_swap(piece)
            (piece,) = call(
                column_kernel, [f32(row_count, 24, LANES)], [column, vector, vector], args=3
            )(got, scores, row_mass)
    sent, raw, text_dual = call(
        last_row_kernel,
        [f32(columns, 24, LANES), f32(big, width), f32(SUB, LANES)],
        [pltpu.VMEM((big // 4, big), jnp.bfloat16)] * 4,
        flops=flops,
        args=4,
    )(got_row, scores, column_mass, t)
    got = column_swap(sent)
    carried, other, speech_dual = call(
        first_cross_kernel,
        [bf16(big, width), bf16(width // 2, width), f32(SUB, LANES)],
        [column],
        flops=flops // 2,
        args=6,
    )(got, sent, got_row, row_mass, raw, s)
    other = lax.ppermute(other, "row", swap)
    (mine,) = call(second_cross_kernel, [f32(width // 2, width)], flops=flops // 2, args=2)(
        carried, s
    )
    (pair,) = call(pair_kernel, [bf16(width // 2, width)], args=2)(mine, other)
    groups = [
        [r * columns + c for r in range(core, row_count, cores) for c in range(columns)]
        for core in range(cores)
    ]
    count = len(groups[0])
    parts = lax.all_to_all(
        pair.reshape(count, width // 2 // count, width),
        ("row", "col"),
        0,
        0,
        axis_index_groups=groups,
    )
    cross = jnp.sum(parts.astype(jnp.float32), axis=0) * math.sqrt(big * row_count)
    return (cross, speech_dual.reshape(-1), text_dual.reshape(-1))


def solution(mesh):
    return jax.shard_map(
        body,
        mesh=mesh,
        in_specs=(P(("row", "col"), None), P(("row", "col")), P("col", "row"), P("col")),
        out_specs=(P(("row", "col"), None), P("row"), P("col")),
        check_vma=False,
    )
```

```python
import functools
import math

import jax
import jax.numpy as jnp
from jax import lax
from jax.experimental import pallas as pl
from jax.experimental.pallas import tpu as pltpu
from jax.sharding import PartitionSpec as P

ITERS = 3
EPS = 0.5
LANES = 128
SUB = 8
LOG2E = math.log2(math.e)
LIMIT = 24 * 1024 * 1024


def call(kernel, outs, scratch=(), flops=0, reads=0, args=0, aliases={}):
    vmem = pl.BlockSpec(memory_space=pltpu.VMEM)
    return pl.pallas_call(
        kernel,
        out_shape=outs,
        in_specs=[vmem] * args,
        out_specs=[vmem] * len(outs),
        scratch_shapes=list(scratch),
        input_output_aliases=aliases,
        compiler_params=pltpu.CompilerParams(vmem_limit_bytes=LIMIT),
        cost_estimate=pl.CostEstimate(flops=flops, bytes_accessed=reads, transcendentals=0),
    )


def f32(*shape):
    return jax.ShapeDtypeStruct(shape, jnp.float32)


def bf16(*shape):
    return jax.ShapeDtypeStruct(shape, jnp.bfloat16)


def total_of(x):
    return jnp.sum(jnp.sum(x, axis=1, keepdims=True), axis=0, keepdims=True)


def combine(got_ref):
    tops = got_ref[:, 0:SUB, :]
    best = jnp.max(tops, axis=0)
    mass = jnp.sum(got_ref[:, SUB : 2 * SUB, :] * jnp.exp2(tops - best[None]), axis=0)
    whole = jnp.sum(got_ref[:, 2 * SUB : 3 * SUB, :], axis=0)
    return best, mass, whole


def send(out_ref, top, mass, whole):
    whole = jnp.broadcast_to(whole, (SUB, LANES))
    for peer in range(out_ref.shape[0]):
        out_ref[peer, 0:SUB, :] = top
        out_ref[peer, SUB : 2 * SUB, :] = mass
        out_ref[peer, 2 * SUB : 3 * SUB, :] = whole


def spread(v, out_ref):
    turned = jnp.concatenate([v, jnp.zeros((LANES - SUB, LANES), jnp.float32)], axis=0).T
    for b in range(SUB):
        out_ref[b * LANES : (b + 1) * LANES, :] = jnp.broadcast_to(
            turned[:, b : b + 1], (LANES, LANES)
        )


def column_stats(scores_ref, rows_ref, top_ref, mass_ref):
    for b in range(SUB):
        values = scores_ref[:, b * LANES : (b + 1) * LANES] + rows_ref[...]
        top = jnp.max(values, axis=0, keepdims=True)
        top_ref[b : b + 1, :] = top
        mass_ref[b : b + 1, :] = jnp.sum(jnp.exp2(values - top), axis=0, keepdims=True)


def row_stats(scores_ref, v, use=None):
    lane = lax.broadcasted_iota(jnp.int32, (LANES, LANES), 1)
    shift = jnp.concatenate([v[b : b + 1, :] for b in range(SUB)], axis=1)
    both = jnp.zeros((LANES, LANES), jnp.float32)
    for b in range(SUB):
        values = scores_ref[b * LANES : (b + 1) * LANES, :] + shift
        top = jnp.max(values, axis=1, keepdims=True)
        weights = jnp.exp2(values - top)
        mass = jnp.sum(weights, axis=1, keepdims=True)
        both = jnp.where(lane == b, top, both)
        both = jnp.where(lane == SUB + b, mass, both)
        if use is not None:
            use(b, weights)
    turned = both.T
    return turned[0:SUB, :], turned[SUB : 2 * SUB, :]


def pack_kernel(speech_ref, mass_ref, piece_ref):
    rows, width = speech_ref.shape
    blocks = width // LANES
    rest = jnp.concatenate([mass_ref[...], mass_ref[...]], axis=1)
    line = lax.broadcasted_iota(jnp.int32, (16, LANES), 0)
    tail = jnp.zeros((16, LANES), jnp.float32)
    for k in range(3):
        term = rest.astype(jnp.bfloat16).astype(jnp.float32)
        tail = jnp.where(line == k, term, tail)
        rest = rest - term
    for lt in range(blocks):
        piece_ref[lt * rows : (lt + 1) * rows, :] = speech_ref[:, lt * LANES : (lt + 1) * LANES]
    piece_ref[blocks * rows :, :] = tail.astype(jnp.bfloat16)


def place_kernel(*refs):
    slice_refs, t_ref = refs[:-1], refs[-1]
    here = lax.axis_index("row")
    blocks = t_ref.shape[0]
    chips = blocks // 2
    for k in range(blocks):
        t_ref[lax.rem(here // 2 + chips - k // 2, chips) * 2 + lax.rem(here + k, 2)] = slice_refs[k][...]


def join_kernel(*refs):
    for k, piece_ref in enumerate(refs[:-1]):
        refs[-1][k] = piece_ref[...]


def lines_kernel(scale, rows, steps, first, last, *refs):
    line_refs, t_ref, refs = refs[: len(steps)], refs[len(steps)], refs[len(steps) + 1 :]
    if first:
        held_ref, stats_ref = None, None
    else:
        held_ref, stats_ref = refs[2:4]
        refs = refs[4:]
    if last:
        scores_ref, s_ref, mass_ref, out_ref, new_held_ref, new_stats_ref, column_ref = refs
    else:
        scores_ref, s_ref, new_held_ref, new_stats_ref, column_ref = refs
    side = line_refs[0].shape[0]
    blocks = t_ref.shape[0]
    core = lax.rem(lax.axis_index("row"), 2)
    here = lax.axis_index("col")
    x, z = here // side, lax.rem(here, side)
    lane = lax.broadcasted_iota(jnp.int32, (1, LANES), 1)
    base = blocks * rows

    def origin(step, k):
        back_x = step + core * (k - step)
        back_z = k + core * (step - k)
        return lax.rem(x + side - back_x, side) * side + lax.rem(z + side - back_z, side)

    pieces = [
        (origin(step, k), line_ref.at[k])
        for step, line_ref in zip(steps, line_refs, strict=True)
        for k in range(side)
    ]
    if not first:
        new_held_ref[...] = held_ref[...]
    masses = []
    for c, piece_ref in pieces:
        terms = piece_ref[base : base + 16, :].astype(jnp.float32)
        masses.append(terms[0:1, :] + terms[1:2, :] + terms[2:3, :])
        new_held_ref[pl.ds(c, 1), :] = masses[-1]
        place = pl.ds(pl.multiple_of(c * rows, rows), rows)
        for lt in range(blocks):
            s_ref[lt, place, :] = piece_ref[lt * rows : (lt + 1) * rows, :]
    empty = jnp.zeros((LANES - len(pieces), LANES), jnp.float32)
    turned = jnp.concatenate([jnp.log2(jnp.concatenate(masses, axis=0)), empty], axis=0).T
    for k in range(len(pieces)):
        column_ref[k * rows : (k + 1) * rows, :] = jnp.broadcast_to(
            turned[0:rows, k : k + 1], (rows, LANES)
        )
    whole = jnp.concatenate(
        [
            jnp.concatenate(
                [piece_ref[lt * rows : (lt + 1) * rows, :] for _, piece_ref in pieces], axis=0
            )
            for lt in range(blocks)
        ],
        axis=1,
    )
    for n in range(4):
        text = jnp.concatenate([t_ref[lt, n * 256 : (n + 1) * 256, :] for lt in range(blocks)], axis=1)
        product = scale * lax.dot_general(
            whole, text, (((1,), (1,)), ((), ())), preferred_element_type=jnp.float32
        )
        for k, (c, _) in enumerate(pieces):
            place = pl.ds(pl.multiple_of(c * rows, rows), rows)
            scores_ref[place, n * 256 : (n + 1) * 256] = product[k * rows : (k + 1) * rows, :]
        for b in (2 * n, 2 * n + 1):
            values = product[:, (b - 2 * n) * LANES : (b - 2 * n + 1) * LANES] + column_ref[...]
            top = jnp.max(values, axis=0, keepdims=True)
            mass = jnp.sum(jnp.exp2(values - top), axis=0, keepdims=True)
            if not first:
                old_top, old_mass = stats_ref[b : b + 1, :], stats_ref[SUB + b : SUB + b + 1, :]
                best = jnp.maximum(top, old_top)
                mass = mass * jnp.exp2(top - best) + old_mass * jnp.exp2(old_top - best)
                top = best
            new_stats_ref[b : b + 1, :] = top
            new_stats_ref[SUB + b : SUB + b + 1, :] = mass
    if last:
        for b in range(SUB):
            mass_ref[b : b + 1, :] = jnp.where(
                lane < rows, new_held_ref[2 * b : 2 * b + 1, :], new_held_ref[2 * b + 1 : 2 * b + 2, :]
            )
        send(out_ref, new_stats_ref[0:SUB, :], new_stats_ref[SUB : 2 * SUB, :], total_of(mass_ref[...]))


def row_kernel(got_ref, scores_ref, mass_ref, out_ref):
    best, mass, whole = combine(got_ref)
    dual = jnp.log2(whole) - (best + jnp.log2(mass))
    top, mass = row_stats(scores_ref, dual + jnp.log2(mass_ref[...]))
    send(out_ref, top, mass, total_of(mass_ref[...]))


def last_row_kernel(
    got_ref, scores_ref, mass_ref, t_ref, out_ref, raw_ref, dual_ref, *weights_refs
):
    best, mass, whole = combine(got_ref)
    dual = jnp.log2(whole) - (best + jnp.log2(mass))
    dual_ref[...] = dual * (EPS / LOG2E)

    text = jnp.concatenate([t_ref[lt] for lt in range(t_ref.shape[0])], axis=1)


    def product(k):
        raw_ref[k * 256 : (k + 1) * 256, :] = jnp.dot(
            weights_refs[k][...], text, preferred_element_type=jnp.float32
        )

    def use(b, weights):
        rows = slice((b % 2) * LANES, (b % 2 + 1) * LANES)
        weights_refs[b // 2][rows, :] = weights.astype(jnp.bfloat16)
        if b % 2 == 1 and b > 1:
            product(b // 2 - 1)

    top, mass = row_stats(scores_ref, dual + jnp.log2(mass_ref[...]), use)
    product(3)
    send(out_ref, top, mass, total_of(mass_ref[...]))


def column_kernel(got_ref, scores_ref, mass_ref, out_ref, rows_ref, a_ref, b_ref):
    best, mass, whole = combine(got_ref)
    dual = jnp.log2(whole) - (best + jnp.log2(mass))
    spread(dual + jnp.log2(mass_ref[...]), rows_ref)
    column_stats(scores_ref, rows_ref, a_ref, b_ref)
    send(out_ref, a_ref[...], b_ref[...], total_of(mass_ref[...]))


def half_cross(s_ref, part, carried):
    left = jnp.concatenate([s_ref[2 * k + part] for k in range(s_ref.shape[0] // 2)], axis=1)
    return lax.dot_general(
        left, carried, (((0,), (0,)), ((), ())), preferred_element_type=jnp.float32
    )


def first_cross_kernel(
    got_ref, sent_ref, row_got_ref, mass_ref, raw_ref, s_ref,
    carried_ref, other_ref, dual_ref, rows_ref,
):
    best, mass, whole = combine(got_ref)
    dual_ref[...] = (jnp.log2(whole) - (best + jnp.log2(mass))) * (EPS / LOG2E)
    speech_total = jnp.sum(row_got_ref[:, 2 * SUB : 3 * SUB, :], axis=0)
    factor = (mass_ref[...] / speech_total) * jnp.exp2(sent_ref[0, 0:SUB, :] - best) / mass
    spread(factor, rows_ref)
    part = 1 - lax.rem(lax.axis_index("row"), 2)

    def product(n):
        lanes = slice(n * 256, (n + 1) * 256)
        other_ref[:, lanes] = half_cross(s_ref, part, carried_ref[:, lanes]).astype(jnp.bfloat16)

    for n in range(4):
        for b in (2 * n, 2 * n + 1):
            carried_ref[:, b * LANES : (b + 1) * LANES] = (
                raw_ref[:, b * LANES : (b + 1) * LANES] * rows_ref[...]
            ).astype(jnp.bfloat16)
        if n > 0:
            product(n - 1)
    product(3)


def second_cross_kernel(
    carried_ref, s_ref, speech_dual_ref, text_dual_ref, out_ref, out_speech_ref, out_text_ref
):
    out_speech_ref[...] = speech_dual_ref[...]
    out_text_ref[...] = text_dual_ref[...]
    out_ref[...] = half_cross(s_ref, lax.rem(lax.axis_index("row"), 2), carried_ref[...])


def pair_kernel(mine_ref, other_ref, out_ref):
    out_ref[...] = (mine_ref[...] + other_ref[...].astype(jnp.float32)).astype(jnp.bfloat16)


def body(speech, speech_mass, text, text_mass):
    rows, width = speech.shape
    columns, row_count = lax.axis_size("col"), lax.axis_size("row")
    cores = 2
    blocks = width // LANES
    big = columns * rows
    flops = 2 * big * big * width

    swap = [(i, i ^ 1) for i in range(row_count)]

    def back(v, k):
        return lax.ppermute(v, "row", [(i, (i + cores * k) % row_count) for i in range(row_count)])

    piece_rows = blocks * rows + 16
    side = 4

    def shift(v, k, swapped):
        moves = []
        for r in range(row_count):
            for x in range(side):
                for z in range(side):
                    to = (x, (z + k) % side) if r % cores == swapped else ((x + k) % side, z)
                    moves.append((r * columns + x * side + z, r * columns + to[0] * side + to[1]))
        return lax.ppermute(v, ("row", "col"), moves)

    (piece,) = call(pack_kernel, [bf16(piece_rows, LANES)], args=2)(
        speech, speech_mass.reshape(1, rows)
    )
    pieces = [piece] + [shift(piece, k, 0) for k in range(1, side)]
    beside = back(text, 1), back(text, 3)
    (line,) = call(join_kernel, [bf16(side, piece_rows, LANES)], args=side)(*pieces)
    late, line = lax.optimization_barrier((text, line))
    lines = [line] + [shift(line, k, 1) for k in range(1, side)]
    slices = [late, beside[0], back(late, 2), beside[1]]
    slices = [v for piece in slices for v in (piece, lax.ppermute(piece, "row", swap))]
    column_mass = text_mass.reshape(SUB, LANES)

    scale = LOG2E / (math.sqrt(width) * EPS)
    vector = pltpu.VMEM((SUB, LANES), jnp.float32)
    column = pltpu.VMEM((big, LANES), jnp.float32)
    (t,) = call(
        place_kernel, [bf16(blocks, big, LANES)], args=row_count
    )(*slices)
    grown = [f32(big, big), bf16(blocks, big, LANES)]
    small = [f32(columns, LANES), f32(2 * SUB, LANES)]
    held = call(
        functools.partial(lines_kernel, scale, rows, (0,), True, False),
        grown + small,
        [pltpu.VMEM((big // side, LANES), jnp.float32)],
        args=2,
    )(lines[0], t)
    held = call(
        functools.partial(lines_kernel, scale, rows, (1, 3), False, False),
        grown + small,
        [pltpu.VMEM((big // 2, LANES), jnp.float32)],
        args=7,
        aliases={3: 0, 4: 1},
    )(lines[1], lines[3], t, *held)
    scores, s, row_mass, piece = call(
        functools.partial(lines_kernel, scale, rows, (2,), False, True),
        grown + [f32(SUB, LANES), f32(row_count, 24, LANES)],
        [pltpu.VMEM(v.shape, v.dtype) for v in small]
        + [pltpu.VMEM((big // side, LANES), jnp.float32)],
        flops=flops // side,
        args=6,
        aliases={2: 0, 3: 1},
    )(lines[2], t, *held)
    row_swap = lambda v: lax.all_to_all(v, "row", 0, 0)
    column_swap = lambda v: lax.all_to_all(v, "col", 0, 0)
    for step in range(ITERS):
        got_row = row_swap(piece)
        if step < ITERS - 1:
            (piece,) = call(row_kernel, [f32(columns, 24, LANES)], args=3)(
                got_row, scores, column_mass
            )
            got = column_swap(piece)
            (piece,) = call(
                column_kernel, [f32(row_count, 24, LANES)], [column, vector, vector], args=3
            )(got, scores, row_mass)
    sent, raw, text_dual = call(
        last_row_kernel,
        [f32(columns, 24, LANES), f32(big, width), f32(SUB, LANES)],
        [pltpu.VMEM((big // 4, big), jnp.bfloat16)] * 4,
        flops=flops,
        args=4,
    )(got_row, scores, column_mass, t)
    got = column_swap(sent)
    carried, other, speech_dual = call(
        first_cross_kernel,
        [bf16(big, width), bf16(width // 2, width), f32(SUB, LANES)],
        [column],
        flops=flops // 2,
        args=6,
    )(got, sent, got_row, row_mass, raw, s)
    other = lax.ppermute(other, "row", swap)
    mine, speech_dual, text_dual = call(
        second_cross_kernel,
        [f32(width // 2, width), f32(SUB, LANES), f32(SUB, LANES)],
        flops=flops // 2,
        args=4,
    )(carried, s, speech_dual, text_dual)
    (pair,) = call(pair_kernel, [bf16(width // 2, width)], args=2)(mine, other)
    groups = [
        [r * columns + c for r in range(core, row_count, cores) for c in range(columns)]
        for core in range(cores)
    ]
    count = len(groups[0])
    parts = lax.all_to_all(
        pair.reshape(count, width // 2 // count, width),
        ("row", "col"),
        0,
        0,
        axis_index_groups=groups,
    )
    cross = jnp.sum(parts.astype(jnp.float32), axis=0) * math.sqrt(big * row_count)
    return (cross, speech_dual.reshape(-1), text_dual.reshape(-1))


def solution(mesh):
    return jax.shard_map(
        body,
        mesh=mesh,
        in_specs=(P(("row", "col"), None), P(("row", "col")), P("col", "row"), P("col")),
        out_specs=(P(("row", "col"), None), P("row"), P("col")),
        check_vma=False,
    )
```

```python
import functools
import math

import jax
import jax.numpy as jnp
from jax import lax
from jax.experimental import pallas as pl
from jax.experimental.pallas import tpu as pltpu
from jax.sharding import PartitionSpec as P

ITERS = 3
EPS = 0.5
LANES = 128
SUB = 8
LOG2E = math.log2(math.e)
LIMIT = 24 * 1024 * 1024


def call(kernel, outs, scratch=(), flops=0, reads=0, args=0, aliases={}):
    vmem = pl.BlockSpec(memory_space=pltpu.VMEM)
    return pl.pallas_call(
        kernel,
        out_shape=outs,
        in_specs=[vmem] * args,
        out_specs=[vmem] * len(outs),
        scratch_shapes=list(scratch),
        input_output_aliases=aliases,
        compiler_params=pltpu.CompilerParams(vmem_limit_bytes=LIMIT),
        cost_estimate=pl.CostEstimate(flops=flops, bytes_accessed=reads, transcendentals=0),
    )


def f32(*shape):
    return jax.ShapeDtypeStruct(shape, jnp.float32)


def bf16(*shape):
    return jax.ShapeDtypeStruct(shape, jnp.bfloat16)


def total_of(x):
    return jnp.sum(jnp.sum(x, axis=1, keepdims=True), axis=0, keepdims=True)


def combine(got_ref):
    tops = got_ref[:, 0:SUB, :]
    best = jnp.max(tops, axis=0)
    mass = jnp.sum(got_ref[:, SUB : 2 * SUB, :] * jnp.exp2(tops - best[None]), axis=0)
    whole = jnp.sum(got_ref[:, 2 * SUB : 3 * SUB, :], axis=0)
    return best, mass, whole


def send(out_ref, top, mass, whole):
    whole = jnp.broadcast_to(whole, (SUB, LANES))
    for peer in range(out_ref.shape[0]):
        out_ref[peer, 0:SUB, :] = top
        out_ref[peer, SUB : 2 * SUB, :] = mass
        out_ref[peer, 2 * SUB : 3 * SUB, :] = whole


def spread(v, out_ref):
    turned = jnp.concatenate([v, jnp.zeros((LANES - SUB, LANES), jnp.float32)], axis=0).T
    for b in range(SUB):
        out_ref[b * LANES : (b + 1) * LANES, :] = jnp.broadcast_to(
            turned[:, b : b + 1], (LANES, LANES)
        )


def column_stats(scores_ref, rows_ref, top_ref, mass_ref):
    for b in range(SUB):
        values = scores_ref[:, b * LANES : (b + 1) * LANES] + rows_ref[...]
        top = jnp.max(values, axis=0, keepdims=True)
        top_ref[b : b + 1, :] = top
        mass_ref[b : b + 1, :] = jnp.sum(jnp.exp2(values - top), axis=0, keepdims=True)


def row_stats(scores_ref, v, use=None):
    lane = lax.broadcasted_iota(jnp.int32, (LANES, LANES), 1)
    shift = jnp.concatenate([v[b : b + 1, :] for b in range(SUB)], axis=1)
    both = jnp.zeros((LANES, LANES), jnp.float32)
    for b in range(SUB):
        values = scores_ref[b * LANES : (b + 1) * LANES, :] + shift
        top = jnp.max(values, axis=1, keepdims=True)
        weights = jnp.exp2(values - top)
        mass = jnp.sum(weights, axis=1, keepdims=True)
        both = jnp.where(lane == b, top, both)
        both = jnp.where(lane == SUB + b, mass, both)
        if use is not None:
            use(b, weights)
    turned = both.T
    return turned[0:SUB, :], turned[SUB : 2 * SUB, :]


def pack_kernel(speech_ref, mass_ref, piece_ref):
    rows, width = speech_ref.shape
    blocks = width // LANES
    rest = jnp.concatenate([mass_ref[...], mass_ref[...]], axis=1)
    line = lax.broadcasted_iota(jnp.int32, (16, LANES), 0)
    tail = jnp.zeros((16, LANES), jnp.float32)
    for k in range(3):
        term = rest.astype(jnp.bfloat16).astype(jnp.float32)
        tail = jnp.where(line == k, term, tail)
        rest = rest - term
    for lt in range(blocks):
        piece_ref[lt * rows : (lt + 1) * rows, :] = speech_ref[:, lt * LANES : (lt + 1) * LANES]
    piece_ref[blocks * rows :, :] = tail.astype(jnp.bfloat16)


def place_kernel(*refs):
    slice_refs, t_ref = refs[:-1], refs[-1]
    here = lax.axis_index("row")
    blocks = t_ref.shape[0]
    chips = blocks // 2
    for k in range(blocks):
        t_ref[lax.rem(here // 2 + chips - k // 2, chips) * 2 + lax.rem(here + k, 2)] = slice_refs[k][...]


def stage_kernel(text_ref, out_ref):
    out_ref[...] = text_ref[...]


def join_kernel(*refs):
    for k, piece_ref in enumerate(refs[:-1]):
        refs[-1][k] = piece_ref[...]


def lines_kernel(scale, rows, steps, first, last, *refs):
    line_refs, t_ref, refs = refs[: len(steps)], refs[len(steps)], refs[len(steps) + 1 :]
    if first:
        held_ref, stats_ref = None, None
    else:
        held_ref, stats_ref = refs[2:4]
        refs = refs[4:]
    if last:
        scores_ref, s_ref, mass_ref, out_ref, new_held_ref, new_stats_ref, column_ref = refs
    else:
        scores_ref, s_ref, new_held_ref, new_stats_ref, column_ref = refs
    side = line_refs[0].shape[0]
    blocks = t_ref.shape[0]
    core = lax.rem(lax.axis_index("row"), 2)
    here = lax.axis_index("col")
    x, z = here // side, lax.rem(here, side)
    lane = lax.broadcasted_iota(jnp.int32, (1, LANES), 1)
    base = blocks * rows

    def origin(step, k):
        back_x = step + core * (k - step)
        back_z = k + core * (step - k)
        return lax.rem(x + side - back_x, side) * side + lax.rem(z + side - back_z, side)

    pieces = [
        (origin(step, k), line_ref.at[k])
        for step, line_ref in zip(steps, line_refs, strict=True)
        for k in range(side)
    ]
    if not first:
        new_held_ref[...] = held_ref[...]
    masses = []
    for c, piece_ref in pieces:
        terms = piece_ref[base : base + 16, :].astype(jnp.float32)
        masses.append(terms[0:1, :] + terms[1:2, :] + terms[2:3, :])
        new_held_ref[pl.ds(c, 1), :] = masses[-1]
        place = pl.ds(pl.multiple_of(c * rows, rows), rows)
        for lt in range(blocks):
            s_ref[lt, place, :] = piece_ref[lt * rows : (lt + 1) * rows, :]
    empty = jnp.zeros((LANES - len(pieces), LANES), jnp.float32)
    turned = jnp.concatenate([jnp.log2(jnp.concatenate(masses, axis=0)), empty], axis=0).T
    for k in range(len(pieces)):
        column_ref[k * rows : (k + 1) * rows, :] = jnp.broadcast_to(
            turned[0:rows, k : k + 1], (rows, LANES)
        )
    whole = jnp.concatenate(
        [
            jnp.concatenate(
                [piece_ref[lt * rows : (lt + 1) * rows, :] for _, piece_ref in pieces], axis=0
            )
            for lt in range(blocks)
        ],
        axis=1,
    )
    for n in range(4):
        text = jnp.concatenate([t_ref[lt, n * 256 : (n + 1) * 256, :] for lt in range(blocks)], axis=1)
        product = scale * lax.dot_general(
            whole, text, (((1,), (1,)), ((), ())), preferred_element_type=jnp.float32
        )
        for k, (c, _) in enumerate(pieces):
            place = pl.ds(pl.multiple_of(c * rows, rows), rows)
            scores_ref[place, n * 256 : (n + 1) * 256] = product[k * rows : (k + 1) * rows, :]
        for b in (2 * n, 2 * n + 1):
            values = product[:, (b - 2 * n) * LANES : (b - 2 * n + 1) * LANES] + column_ref[...]
            top = jnp.max(values, axis=0, keepdims=True)
            mass = jnp.sum(jnp.exp2(values - top), axis=0, keepdims=True)
            if not first:
                old_top, old_mass = stats_ref[b : b + 1, :], stats_ref[SUB + b : SUB + b + 1, :]
                best = jnp.maximum(top, old_top)
                mass = mass * jnp.exp2(top - best) + old_mass * jnp.exp2(old_top - best)
                top = best
            new_stats_ref[b : b + 1, :] = top
            new_stats_ref[SUB + b : SUB + b + 1, :] = mass
    if last:
        for b in range(SUB):
            mass_ref[b : b + 1, :] = jnp.where(
                lane < rows, new_held_ref[2 * b : 2 * b + 1, :], new_held_ref[2 * b + 1 : 2 * b + 2, :]
            )
        send(out_ref, new_stats_ref[0:SUB, :], new_stats_ref[SUB : 2 * SUB, :], total_of(mass_ref[...]))


def row_kernel(got_ref, scores_ref, mass_ref, out_ref):
    best, mass, whole = combine(got_ref)
    dual = jnp.log2(whole) - (best + jnp.log2(mass))
    top, mass = row_stats(scores_ref, dual + jnp.log2(mass_ref[...]))
    send(out_ref, top, mass, total_of(mass_ref[...]))


def last_row_kernel(
    got_ref, scores_ref, mass_ref, t_ref, out_ref, raw_ref, dual_ref, *weights_refs
):
    best, mass, whole = combine(got_ref)
    dual = jnp.log2(whole) - (best + jnp.log2(mass))
    dual_ref[...] = dual * (EPS / LOG2E)

    text = jnp.concatenate([t_ref[lt] for lt in range(t_ref.shape[0])], axis=1)


    def product(k):
        raw_ref[k * 256 : (k + 1) * 256, :] = jnp.dot(
            weights_refs[k][...], text, preferred_element_type=jnp.float32
        )

    def use(b, weights):
        rows = slice((b % 2) * LANES, (b % 2 + 1) * LANES)
        weights_refs[b // 2][rows, :] = weights.astype(jnp.bfloat16)
        if b % 2 == 1 and b > 1:
            product(b // 2 - 1)

    top, mass = row_stats(scores_ref, dual + jnp.log2(mass_ref[...]), use)
    product(3)
    send(out_ref, top, mass, total_of(mass_ref[...]))


def column_kernel(got_ref, scores_ref, mass_ref, out_ref, rows_ref, a_ref, b_ref):
    best, mass, whole = combine(got_ref)
    dual = jnp.log2(whole) - (best + jnp.log2(mass))
    spread(dual + jnp.log2(mass_ref[...]), rows_ref)
    column_stats(scores_ref, rows_ref, a_ref, b_ref)
    send(out_ref, a_ref[...], b_ref[...], total_of(mass_ref[...]))


def half_cross(s_ref, part, carried):
    left = jnp.concatenate([s_ref[2 * k + part] for k in range(s_ref.shape[0] // 2)], axis=1)
    return lax.dot_general(
        left, carried, (((0,), (0,)), ((), ())), preferred_element_type=jnp.float32
    )


def first_cross_kernel(
    got_ref, sent_ref, row_got_ref, mass_ref, raw_ref, s_ref,
    carried_ref, other_ref, dual_ref, rows_ref,
):
    best, mass, whole = combine(got_ref)
    dual_ref[...] = (jnp.log2(whole) - (best + jnp.log2(mass))) * (EPS / LOG2E)
    speech_total = jnp.sum(row_got_ref[:, 2 * SUB : 3 * SUB, :], axis=0)
    factor = (mass_ref[...] / speech_total) * jnp.exp2(sent_ref[0, 0:SUB, :] - best) / mass
    spread(factor, rows_ref)
    part = 1 - lax.rem(lax.axis_index("row"), 2)

    def product(n):
        lanes = slice(n * 256, (n + 1) * 256)
        other_ref[:, lanes] = half_cross(s_ref, part, carried_ref[:, lanes]).astype(jnp.bfloat16)

    for n in range(4):
        for b in (2 * n, 2 * n + 1):
            carried_ref[:, b * LANES : (b + 1) * LANES] = (
                raw_ref[:, b * LANES : (b + 1) * LANES] * rows_ref[...]
            ).astype(jnp.bfloat16)
        if n > 0:
            product(n - 1)
    product(3)


def second_cross_kernel(
    carried_ref, s_ref, speech_dual_ref, text_dual_ref, out_ref, out_speech_ref, out_text_ref
):
    out_speech_ref[...] = speech_dual_ref[...]
    out_text_ref[...] = text_dual_ref[...]
    out_ref[...] = half_cross(s_ref, lax.rem(lax.axis_index("row"), 2), carried_ref[...])


def pair_kernel(mine_ref, other_ref, out_ref):
    out_ref[...] = (mine_ref[...] + other_ref[...].astype(jnp.float32)).astype(jnp.bfloat16)


def body(speech, speech_mass, text, text_mass):
    rows, width = speech.shape
    columns, row_count = lax.axis_size("col"), lax.axis_size("row")
    cores = 2
    blocks = width // LANES
    big = columns * rows
    flops = 2 * big * big * width

    swap = [(i, i ^ 1) for i in range(row_count)]

    def back(v, k):
        return lax.ppermute(v, "row", [(i, (i + cores * k) % row_count) for i in range(row_count)])

    piece_rows = blocks * rows + 16
    side = 4

    def shift(v, k, swapped):
        moves = []
        for r in range(row_count):
            for x in range(side):
                for z in range(side):
                    to = (x, (z + k) % side) if r % cores == swapped else ((x + k) % side, z)
                    moves.append((r * columns + x * side + z, r * columns + to[0] * side + to[1]))
        return lax.ppermute(v, ("row", "col"), moves)

    (piece,) = call(pack_kernel, [bf16(piece_rows, LANES)], args=2)(
        speech, speech_mass.reshape(1, rows)
    )
    pieces = [piece] + [shift(piece, k, 0) for k in range(1, side)]
    beside = back(text, 1), back(text, 3)
    (line,) = call(join_kernel, [bf16(side, piece_rows, LANES)], args=side)(*pieces)
    late, line = lax.optimization_barrier((text, line))
    lines = [line] + [shift(line, k, 1) for k in range(1, side)]
    slices = [late, beside[0], back(late, 2), beside[1]]
    slices = [v for piece in slices for v in (piece, lax.ppermute(piece, "row", swap))]
    own, slices[4] = lax.optimization_barrier((text, slices[4]))
    (slices[0],) = call(stage_kernel, [bf16(*text.shape)], args=1)(own)
    column_mass = text_mass.reshape(SUB, LANES)

    scale = LOG2E / (math.sqrt(width) * EPS)
    vector = pltpu.VMEM((SUB, LANES), jnp.float32)
    column = pltpu.VMEM((big, LANES), jnp.float32)
    (t,) = call(
        place_kernel, [bf16(blocks, big, LANES)], args=row_count
    )(*slices)
    grown = [f32(big, big), bf16(blocks, big, LANES)]
    small = [f32(columns, LANES), f32(2 * SUB, LANES)]
    held = call(
        functools.partial(lines_kernel, scale, rows, (0,), True, False),
        grown + small,
        [pltpu.VMEM((big // side, LANES), jnp.float32)],
        args=2,
    )(lines[0], t)
    held = call(
        functools.partial(lines_kernel, scale, rows, (1, 3), False, False),
        grown + small,
        [pltpu.VMEM((big // 2, LANES), jnp.float32)],
        args=7,
        aliases={3: 0, 4: 1},
    )(lines[1], lines[3], t, *held)
    scores, s, row_mass, piece = call(
        functools.partial(lines_kernel, scale, rows, (2,), False, True),
        grown + [f32(SUB, LANES), f32(row_count, 24, LANES)],
        [pltpu.VMEM(v.shape, v.dtype) for v in small]
        + [pltpu.VMEM((big // side, LANES), jnp.float32)],
        flops=flops // side,
        args=6,
        aliases={2: 0, 3: 1},
    )(lines[2], t, *held)
    row_swap = lambda v: lax.all_to_all(v, "row", 0, 0)
    column_swap = lambda v: lax.all_to_all(v, "col", 0, 0)
    for step in range(ITERS):
        got_row = row_swap(piece)
        if step < ITERS - 1:
            (piece,) = call(row_kernel, [f32(columns, 24, LANES)], args=3)(
                got_row, scores, column_mass
            )
            got = column_swap(piece)
            (piece,) = call(
                column_kernel, [f32(row_count, 24, LANES)], [column, vector, vector], args=3
            )(got, scores, row_mass)
    sent, raw, text_dual = call(
        last_row_kernel,
        [f32(columns, 24, LANES), f32(big, width), f32(SUB, LANES)],
        [pltpu.VMEM((big // 4, big), jnp.bfloat16)] * 4,
        flops=flops,
        args=4,
    )(got_row, scores, column_mass, t)
    got = column_swap(sent)
    carried, other, speech_dual = call(
        first_cross_kernel,
        [bf16(big, width), bf16(width // 2, width), f32(SUB, LANES)],
        [column],
        flops=flops // 2,
        args=6,
    )(got, sent, got_row, row_mass, raw, s)
    other = lax.ppermute(other, "row", swap)
    mine, speech_dual, text_dual = call(
        second_cross_kernel,
        [f32(width // 2, width), f32(SUB, LANES), f32(SUB, LANES)],
        flops=flops // 2,
        args=4,
    )(carried, s, speech_dual, text_dual)
    (pair,) = call(pair_kernel, [bf16(width // 2, width)], args=2)(mine, other)
    groups = [
        [r * columns + c for r in range(core, row_count, cores) for c in range(columns)]
        for core in range(cores)
    ]
    count = len(groups[0])
    parts = lax.all_to_all(
        pair.reshape(count, width // 2 // count, width),
        ("row", "col"),
        0,
        0,
        axis_index_groups=groups,
    )
    cross = jnp.sum(parts.astype(jnp.float32), axis=0) * math.sqrt(big * row_count)
    return (cross, speech_dual.reshape(-1), text_dual.reshape(-1))


def solution(mesh):
    return jax.shard_map(
        body,
        mesh=mesh,
        in_specs=(P(("row", "col"), None), P(("row", "col")), P("col", "row"), P("col")),
        out_specs=(P(("row", "col"), None), P("row"), P("col")),
        check_vma=False,
    )
```
